32 devices in a mesh: feat: 8 (over y, x, core), dom: 4 (over z).
Axes of the slice: x: 2, y: 2, z: 4, core: 2. Of those that a mesh axis runs over, the one named last changes fastest.
Arguments:
- features: bfloat16 [768, 4096], P('feat', 'dom'), may hold values from -6 to 6
- neigh_one: int32 [4, 15, 512], P('dom'), may hold values from 0 to 1023
- boundary: int32 [4, 8, 128], P('dom', 'feat'), may hold values from 0 to 63
- neigh_two: int32 [4, 256, 10], P('dom', 'feat'), may hold values from 0 to 191
- weight_one: bfloat16 [2, 768, 256], P(None, 'feat'), may hold values from -0.21875 to 0.21875
- weight_two: bfloat16 [2, 256, 256], replicated, may hold values from -0.375 to 0.375
Outputs:
- hidden_two: bfloat16 [4, 256, 256], P('dom', 'feat')
The draws below stay inside these ranges and needn't reach their ends.
Inputs may be any that keep to these rules, and one draw needn't show every extreme that they name: `neigh_one`: source node of a partition. `boundary`: local layer-one output row of the sending device. `neigh_two`: row of the device's table.
All inputs are finite; a program needn't handle non-finite values.
Results may differ from the reference program's by a relative error of at most 0.0051.
Values may be sent and summed in bfloat16 or wider, within the bound.
No kernel may reach another device: no remote copies, remote signals or barrier semaphores. Data moves between devices by JAX's collectives and lax.ppermute only.
A program may use at most 64 MiB of HBM per device.

```python
import jax
import jax.numpy as jnp
from jax import lax

FEAT = 768
HID = 256
FAN1 = 15
FAN2 = 10
R1 = 64
BND = 32
R2 = 32
DSTP = 512
SRCP = 1024
N_FEAT = 8
N_DOM = 4


def with_ends(result, rng, smallest, largest):
    longest = result.shape.index(max(result.shape))
    spots = []
    for shift in (0, 1):
        where = [jax.random.randint(jax.random.fold_in(rng, axis), (), 0, length) for axis, length in enumerate(result.shape)]
        where[longest] = (where[longest] + shift) % result.shape[longest]
        spots.append(tuple(where))
    return result.at[spots[0]].set(smallest).at[spots[1]].set(largest)


def block_levels(own_key, shape, cuts, smallest, top_value):
    def one(dim, blocks):
        heights = jax.random.uniform(jax.random.fold_in(jax.random.fold_in(own_key, 6), dim), (blocks,), jnp.float32, smallest / len(cuts), top_value / len(cuts))
        return jnp.repeat(jnp.exp(heights), shape[dim] // blocks).reshape((-1,) + (1,) * (len(shape) - dim - 1))

    level = one(*cuts[0])
    for cut in cuts[1:]:
        level = level * one(*cut)
    return level


def scatter_about(own_key, shape, spread, limit, shards=(), kind=jnp.bfloat16):
    drawn = spread * jax.random.normal(own_key, shape, jnp.float32)
    if shards:
        drawn = drawn * block_levels(own_key, shape, shards, -0.22, 0.18)
    return jnp.clip(drawn, -limit, limit).astype(kind)


def setup_inputs(seed: int = 0) -> dict:
    keys = jax.random.split(jax.random.key(seed), 7)
    return {
        "features": scatter_about(keys[0], (FEAT, N_DOM * SRCP), 1.0, 6.0, ((0, 8), (1, 4))),
        "neigh_one": with_ends(jax.random.randint(keys[1], (N_DOM, FAN1, DSTP), 0, SRCP), jax.random.fold_in(keys[1], 1), 0, SRCP - 1).astype(jnp.int32),
        "boundary": with_ends(jax.random.randint(keys[2], (N_DOM, N_FEAT, N_DOM * BND), 0, R1), jax.random.fold_in(keys[2], 1), 0, R1 - 1).astype(jnp.int32),
        "neigh_two": with_ends(jax.random.randint(keys[3], (N_DOM, N_FEAT * R2, FAN2), 0, R1 + N_DOM * BND), jax.random.fold_in(keys[3], 1), 0, (R1 + N_DOM * BND) - 1).astype(jnp.int32),
        "weight_one": scatter_about(keys[4], (2, FEAT, HID), FEAT ** -0.5, 0.21875, ((1, 8),)),
        "weight_two": scatter_about(keys[5], (2, HID, HID), HID ** -0.5, 0.375),
    }


def layer_one(columns, neigh, weight_one):
    def add_one(total, index):
        return total + jnp.take(columns, index, axis=1).astype(jnp.float32), None

    start = jnp.zeros((columns.shape[0], neigh.shape[1]), jnp.float32)
    summed, _ = lax.scan(add_one, start, neigh)
    agg = (summed / FAN1).astype(jnp.bfloat16)
    own = columns[:, :neigh.shape[1]]
    dims = (((0,), (0,)), ((), ()))
    pre = lax.dot_general(own, weight_one[0], dims, preferred_element_type=jnp.float32)
    pre = pre + lax.dot_general(agg, weight_one[1], dims, preferred_element_type=jnp.float32)
    return jax.nn.relu(pre).astype(jnp.bfloat16)


def reference(features, neigh_one, boundary, neigh_two, weight_one, weight_two):
    parts = features.reshape(FEAT, N_DOM, SRCP).transpose(1, 0, 2)
    hidden = jnp.stack([layer_one(parts[d], neigh_one[d], weight_one) for d in range(N_DOM)])
    local = hidden.reshape(N_DOM, N_FEAT, R1, HID)
    sends = boundary.reshape(N_DOM, N_FEAT, N_DOM * BND)
    picked = jax.vmap(jax.vmap(lambda rows, index: rows[index]))(local, sends)
    picked = picked.reshape(N_DOM, N_FEAT, N_DOM, BND, HID)
    recv = picked.transpose(2, 1, 0, 3, 4).reshape(N_DOM, N_FEAT, N_DOM * BND, HID)
    table = jnp.concatenate([local, recv], axis=2)
    neigh = neigh_two.reshape(N_DOM, N_FEAT, R2, FAN2)

    def one_device(rows, index, own):
        summed = jnp.zeros((R2, HID), jnp.float32)
        for k in range(FAN2):
            summed = summed + rows[index[:, k]].astype(jnp.float32)
        agg = (summed / FAN2).astype(jnp.bfloat16)
        pre = jnp.dot(own[:R2], weight_two[0], preferred_element_type=jnp.float32)
        pre = pre + jnp.dot(agg, weight_two[1], preferred_element_type=jnp.float32)
        return jax.nn.relu(pre).astype(jnp.bfloat16)

    out = jax.vmap(jax.vmap(one_device))(table, neigh, local)
    return out.reshape(N_DOM, N_FEAT * R2, HID)
```

```python
import math

import jax
import jax.numpy as jnp
from jax import lax
from jax.experimental import pallas as pl
from jax.experimental.pallas import tpu as pltpu
from jax.sharding import PartitionSpec as P

FAN1 = 15
FAN2 = 10
CHUNK = 256
COLUMNS_FIRST = (((0,), (0,)), ((), ()))


def counts_of(rows, start, height):
    width = rows[0].shape[1]
    slots = lax.broadcasted_iota(jnp.int32, (height, width), 0).astype(jnp.float32).astype(jnp.bfloat16)
    one = jnp.ones((), jnp.bfloat16)
    zero = jnp.zeros((), jnp.bfloat16)
    counts = None
    for row in rows:
        near = (row - start).astype(jnp.float32).astype(jnp.bfloat16)
        hit = jnp.where(near == slots, one, zero)
        counts = hit if counts is None else counts + hit
    return counts


def partial_kernel(features, own, neigh, weight, partial):
    fan = neigh.shape[0]
    sources = features.shape[1]
    chunk = min(CHUNK, sources)
    rows = [neigh[k] for k in range(fan)]

    def summed_over(start):
        counts = counts_of(rows, start, chunk)
        return jnp.dot(features[:, pl.ds(start, chunk)], counts, preferred_element_type=jnp.float32)

    if sources // chunk <= 8:
        total = summed_over(0)
        for step in range(1, sources // chunk):
            total = total + summed_over(step * chunk)
    else:
        total = lax.fori_loop(
            0,
            sources // chunk,
            lambda step, so_far: so_far + summed_over(pl.multiple_of(step * chunk, chunk)),
            jnp.zeros((features.shape[0], rows[0].shape[1]), jnp.float32),
        )
    agg = (total / FAN1).astype(jnp.bfloat16)
    pre = lax.dot_general(own[...], weight[0], COLUMNS_FIRST, preferred_element_type=jnp.float32)
    pre = pre + lax.dot_general(agg, weight[1], COLUMNS_FIRST, preferred_element_type=jnp.float32)
    partial[...] = pre.astype(partial.dtype)


def partial_sums(features, neigh, weight):
    fan, _, nodes = neigh.shape
    depth, sources = features.shape
    width = weight.shape[2]
    block = math.gcd(nodes, 512)
    return pl.pallas_call(
        partial_kernel,
        out_shape=jax.ShapeDtypeStruct((nodes, width), jnp.bfloat16),
        grid=(nodes // block,),
        in_specs=[
            pl.BlockSpec((depth, sources), lambda i: (0, 0)),
            pl.BlockSpec((depth, block), lambda i: (0, i)),
            pl.BlockSpec((fan, 1, block), lambda i: (0, 0, i)),
            pl.BlockSpec((2, depth, width), lambda i: (0, 0, 0)),
        ],
        out_specs=pl.BlockSpec((block, width), lambda i: (i, 0)),
        name="layer_one_partial_sums",
    )(features, features, neigh, weight)


def hidden_kernel(partials, boundary, hidden, picked):
    pre = partials[0].astype(jnp.float32)
    for part in range(1, partials.shape[0]):
        pre = pre + partials[part].astype(jnp.float32)
    rows = jnp.maximum(pre, 0.0).astype(jnp.bfloat16)
    hidden[...] = rows
    chosen = counts_of([boundary[0]], 0, rows.shape[0])
    picked[...] = lax.dot_general(
        chosen, rows, COLUMNS_FIRST, preferred_element_type=jnp.float32
    ).astype(jnp.bfloat16)


def layer_two_kernel(hidden, incoming, neigh, weight, out):
    rows = [neigh[k] for k in range(neigh.shape[0])]
    local = hidden.shape[0]
    out_rows = rows[0].shape[1]
    total = lax.dot_general(
        counts_of(rows, 0, local), hidden[...], COLUMNS_FIRST, preferred_element_type=jnp.float32
    )
    far = incoming.shape[0]
    step = min(far, 256)
    for start in range(0, far, step):
        counts = counts_of(rows, local + start, step)
        total = total + lax.dot_general(
            counts, incoming[pl.ds(start, step), :], COLUMNS_FIRST, preferred_element_type=jnp.float32
        )
    agg = (total / FAN2).astype(jnp.bfloat16)
    result = jnp.dot(hidden[pl.ds(0, out_rows), :], weight[0], preferred_element_type=jnp.float32)
    result = result + jnp.dot(agg, weight[1], preferred_element_type=jnp.float32)
    out[0] = jnp.maximum(result, 0.0).astype(jnp.bfloat16)


def on_device(features, neigh_one, boundary, neigh_two, weight_one, weight_two):
    width = weight_one.shape[2]
    partial = partial_sums(features, neigh_one.transpose(1, 0, 2), weight_one)
    feat_count = lax.axis_size("feat")
    partials = lax.all_to_all(partial, "feat", split_axis=0, concat_axis=0, tiled=True)
    partials = partials.reshape(feat_count, -1, width)
    local = partials.shape[1]
    sent = boundary.shape[2]
    hidden, picked = pl.pallas_call(
        hidden_kernel,
        out_shape=(
            jax.ShapeDtypeStruct((local, width), jnp.bfloat16),
            jax.ShapeDtypeStruct((sent, width), jnp.bfloat16),
        ),
        name="hidden_and_boundary_rows",
    )(partials, boundary)
    incoming = lax.all_to_all(picked, "dom", split_axis=0, concat_axis=0, tiled=True)
    return pl.pallas_call(
        layer_two_kernel,
        out_shape=jax.ShapeDtypeStruct((1, neigh_two.shape[1], weight_two.shape[2]), jnp.bfloat16),
        name="layer_two",
    )(hidden, incoming, neigh_two.transpose(2, 0, 1), weight_two)


def solution(mesh):
    placed = (
        P("feat", "dom"),
        P("dom", None, None),
        P("dom", "feat", None),
        P("dom", "feat", None),
        P(None, "feat", None),
        P(),
    )
    return jax.shard_map(
        on_device, mesh=mesh, in_specs=placed, out_specs=P("dom", "feat", None), check_vma=False
    )
```

```python
import math

import jax
import jax.numpy as jnp
from jax import lax
from jax.experimental import pallas as pl
from jax.experimental.pallas import tpu as pltpu
from jax.sharding import PartitionSpec as P

FAN1 = 15
FAN2 = 10
CHUNK = 256
COLUMNS_FIRST = (((0,), (0,)), ((), ()))
VMEM = pl.BlockSpec(memory_space=pltpu.VMEM)


def f32_dot(a, b):
    return jnp.dot(a, b, preferred_element_type=jnp.float32)


def f32_dot_columns(a, b):
    return lax.dot_general(a, b, COLUMNS_FIRST, preferred_element_type=jnp.float32)


def counts_of(rows, start, height):
    width = rows[0].shape[1]
    slots = lax.broadcasted_iota(jnp.int32, (height, width), 0).astype(jnp.float32).astype(jnp.bfloat16)
    one = jnp.ones((), jnp.bfloat16)
    zero = jnp.zeros((), jnp.bfloat16)
    counts = None
    for row in rows:
        near = (row - start).astype(jnp.float32).astype(jnp.bfloat16)
        hit = jnp.where(near == slots, one, zero)
        counts = hit if counts is None else counts + hit
    return counts


def counts_kernel(neigh, counts):
    core = lax.rem(lax.axis_index("feat"), 2)
    index = neigh[:, 0, :]
    lane = lax.broadcasted_iota(jnp.int32, (index.shape[0], 128), 1)
    groups = []
    for start in range(0, index.shape[1], 256):
        a = index[:, start : start + 128]
        b = index[:, start + 128 : start + 256]
        first = jnp.where(core == 0, a, pltpu.roll(a, 64, 1))
        second = jnp.where(core == 0, pltpu.roll(b, 64, 1), b)
        groups.append(jnp.where(lane < 64, first, second))
    index = jnp.concatenate(groups, axis=1)
    rows = [index[k : k + 1] for k in range(index.shape[0])]
    chunk = min(CHUNK, counts.shape[0])
    for start in range(0, counts.shape[0], chunk):
        counts[pl.ds(start, chunk), :] = counts_of(rows, start, chunk)


def sums_kernel(mine, theirs, counts, weight, their_weight, kept, *rest):
    sent, own_all, agg_all = rest[:-2], rest[-2], rest[-1]
    me = lax.axis_index("feat")
    core, chip = lax.rem(me, 2), lax.div(me, 2)
    nodes = own_all.shape[0]
    local = kept.shape[0]
    own_all[...] = f32_dot_columns(mine[:, :nodes], weight[0]) + f32_dot_columns(
        theirs[:, :nodes], their_weight[0]
    )
    agg = (f32_dot(mine[...], counts[...]) / FAN1).astype(jnp.bfloat16)
    their_agg = (f32_dot(theirs[...], counts[...]) / FAN1).astype(jnp.bfloat16)
    agg_all[...] = f32_dot_columns(agg, weight[1]) + f32_dot_columns(their_agg, their_weight[1])
    for apart in range(len(sent) + 1):
        to = jnp.bitwise_xor(chip, apart)
        own = own_all[pl.ds(pl.multiple_of((2 * to + core) * local, local), local), :]
        pre = own + agg_all[pl.ds(pl.multiple_of(to * local, local), local), :]
        if apart == 0:
            kept[...] = pre
        else:
            sent[apart - 1][...] = pre.astype(jnp.bfloat16)


def rows_kernel(kept, *rest):
    partials, boundary, hidden, near, sent, picked = rest[:-7], rest[-7], rest[-6], rest[-5], rest[-4:-1], rest[-1]
    me = lax.axis_index("dom")
    pre = kept[...]
    for part in partials:
        pre = pre + part[...].astype(jnp.float32)
    rows = jnp.maximum(pre, 0.0).astype(jnp.bfloat16)
    hidden[...] = rows
    picked[...] = f32_dot_columns(counts_of([boundary[0]], 0, rows.shape[0]), rows).astype(jnp.bfloat16)
    share = near.shape[0]
    for apart, to in enumerate((near, *sent)):
        start = pl.multiple_of(jnp.bitwise_xor(me, apart) * share, share)
        to[...] = picked[pl.ds(start, share), :]


def near_kernel(hidden, near, neigh, weight, base, total, counts):
    me = lax.axis_index("dom")
    rows = [neigh[k] for k in range(neigh.shape[0])]
    local, share, out_rows = hidden.shape[0], near.shape[0], base.shape[0]
    base[...] = f32_dot(hidden[pl.ds(0, out_rows), :], weight[0])
    total[...] = f32_dot_columns(counts_of(rows, 0, local), hidden[...]) + f32_dot_columns(
        counts_of(rows, local + me * share, share), near[...]
    )
    for apart in range(1, counts.shape[0] + 1):
        start = local + jnp.bitwise_xor(me, apart) * share
        counts[apart - 1] = counts_of(rows, start, share)


def far_kernel(base, total, counts, *rest):
    incoming, weight, out = rest[:-2], rest[-2], rest[-1]
    summed = total[...]
    for part, rows in enumerate(incoming):
        summed = summed + f32_dot_columns(counts[part], rows[...])
    agg = (summed / FAN2).astype(jnp.bfloat16)
    out[0] = jnp.maximum(base[...] + f32_dot(agg, weight[1]), 0.0).astype(jnp.bfloat16)


def call(kernel, outs, operands, name, scratch=(), flops=0):
    return pl.pallas_call(
        kernel,
        out_shape=outs,
        in_specs=[VMEM] * len(operands),
        out_specs=jax.tree.map(lambda _: VMEM, outs),
        scratch_shapes=scratch,
        compiler_params=pltpu.CompilerParams(vmem_limit_bytes=8 << 20),
        name=name,
    )(*operands)


def apart_by(count, step):
    return [(i, i ^ step) for i in range(count)]


def on_small_mesh(features, neigh_one, boundary, neigh_two, weight_one, weight_two):
    feat_count, dom_count = lax.axis_size("feat"), lax.axis_size("dom")
    width = weight_one.shape[2]
    nodes = neigh_one.shape[2]
    local = nodes // feat_count
    share = boundary.shape[2] // dom_count
    out_rows = neigh_two.shape[1]
    shape = jax.ShapeDtypeStruct
    bf16, f32 = jnp.bfloat16, jnp.float32

    theirs = lax.ppermute(features, "feat", apart_by(feat_count, 1))
    their_weight = lax.ppermute(weight_one, "feat", apart_by(feat_count, 1))
    counts = call(
        counts_kernel, shape((features.shape[1], nodes // 2), bf16), [neigh_one.transpose(1, 0, 2)], "layer_one_counts"
    )
    chips = feat_count // 2
    kept, *sent = call(
        sums_kernel,
        (shape((local, width), f32),) + (shape((local, width), bf16),) * (chips - 1),
        [features, theirs, counts, weight_one, their_weight],
        "layer_one_sums",
        scratch=[pltpu.VMEM((nodes, width), f32), pltpu.VMEM((nodes // 2, width), f32)],
    )
    partials = [lax.ppermute(rows, "feat", apart_by(feat_count, 2 * (k + 1))) for k, rows in enumerate(sent)]
    hidden, near, *sent = call(
        rows_kernel,
        (shape((local, width), bf16),) + (shape((share, width), bf16),) * dom_count,
        [kept, *partials, boundary],
        "hidden_and_boundary_rows",
        scratch=[pltpu.VMEM((share * dom_count, width), bf16)],
    )
    incoming = [lax.ppermute(rows, "dom", apart_by(dom_count, k + 1)) for k, rows in enumerate(sent)]
    index_two = neigh_two.transpose(2, 0, 1)
    base, total, counts_two = call(
        near_kernel,
        (
            shape((out_rows, width), f32),
            shape((out_rows, width), f32),
            shape((dom_count - 1, share, out_rows), bf16),
        ),
        [hidden, near, index_two, weight_two],
        "layer_two_near",
    )
    return call(
        far_kernel,
        shape((1, out_rows, weight_two.shape[2]), bf16),
        [base, total, counts_two, *incoming, weight_two],
        "layer_two_far",
    )


def partial_kernel(features, own, neigh, weight, partial):
    fan = neigh.shape[0]
    sources = features.shape[1]
    chunk = min(CHUNK, sources)
    rows = [neigh[k] for k in range(fan)]

    def add_chunk(step, so_far):
        start = pl.multiple_of(step * chunk, chunk)
        return so_far + f32_dot(features[:, pl.ds(start, chunk)], counts_of(rows, start, chunk))

    total = lax.fori_loop(
        0, sources // chunk, add_chunk, jnp.zeros((features.shape[0], rows[0].shape[1]), jnp.float32)
    )
    agg = (total / FAN1).astype(jnp.bfloat16)
    pre = f32_dot_columns(own[...], weight[0]) + f32_dot_columns(agg, weight[1])
    partial[...] = pre.astype(partial.dtype)


def partial_sums(features, neigh, weight):
    fan, _, nodes = neigh.shape
    depth, sources = features.shape
    width = weight.shape[2]
    block = math.gcd(nodes, 512)
    return pl.pallas_call(
        partial_kernel,
        out_shape=jax.ShapeDtypeStruct((nodes, width), jnp.bfloat16),
        grid=(nodes // block,),
        in_specs=[
            pl.BlockSpec((depth, sources), lambda i: (0, 0)),
            pl.BlockSpec((depth, block), lambda i: (0, i)),
            pl.BlockSpec((fan, 1, block), lambda i: (0, 0, i)),
            pl.BlockSpec((2, depth, width), lambda i: (0, 0, 0)),
        ],
        out_specs=pl.BlockSpec((block, width), lambda i: (i, 0)),
        name="layer_one_partial_sums",
    )(features, features, neigh, weight)


def hidden_kernel(partials, boundary, hidden, picked):
    pre = partials[0].astype(jnp.float32)
    for part in range(1, partials.shape[0]):
        pre = pre + partials[part].astype(jnp.float32)
    rows = jnp.maximum(pre, 0.0).astype(jnp.bfloat16)
    hidden[...] = rows
    picked[...] = f32_dot_columns(counts_of([boundary[0]], 0, rows.shape[0]), rows).astype(jnp.bfloat16)


def layer_two_kernel(hidden, incoming, neigh, weight, out):
    rows = [neigh[k] for k in range(neigh.shape[0])]
    local = hidden.shape[0]
    out_rows = rows[0].shape[1]
    total = f32_dot_columns(counts_of(rows, 0, local), hidden[...])
    far = incoming.shape[0]
    step = math.gcd(far, 256)
    for start in range(0, far, step):
        total = total + f32_dot_columns(
            counts_of(rows, local + start, step), incoming[pl.ds(start, step), :]
        )
    agg = (total / FAN2).astype(jnp.bfloat16)
    result = f32_dot(hidden[pl.ds(0, out_rows), :], weight[0]) + f32_dot(agg, weight[1])
    out[0] = jnp.maximum(result, 0.0).astype(jnp.bfloat16)


def on_any_mesh(features, neigh_one, boundary, neigh_two, weight_one, weight_two):
    width = weight_one.shape[2]
    partial = partial_sums(features, neigh_one.transpose(1, 0, 2), weight_one)
    feat_count = lax.axis_size("feat")
    partials = lax.all_to_all(partial, "feat", split_axis=0, concat_axis=0, tiled=True)
    partials = partials.reshape(feat_count, -1, width)
    hidden, picked = pl.pallas_call(
        hidden_kernel,
        out_shape=(
            jax.ShapeDtypeStruct((partials.shape[1], width), jnp.bfloat16),
            jax.ShapeDtypeStruct((boundary.shape[2], width), jnp.bfloat16),
        ),
        name="hidden_and_boundary_rows",
    )(partials, boundary)
    incoming = lax.all_to_all(picked, "dom", split_axis=0, concat_axis=0, tiled=True)
    return pl.pallas_call(
        layer_two_kernel,
        out_shape=jax.ShapeDtypeStruct((1, neigh_two.shape[1], weight_two.shape[2]), jnp.bfloat16),
        name="layer_two",
    )(hidden, incoming, neigh_two.transpose(2, 0, 1), weight_two)


def solution(mesh):
    placed = (
        P("feat", "dom"),
        P("dom", None, None),
        P("dom", "feat", None),
        P("dom", "feat", None),
        P(None, "feat", None),
        P(),
    )
    on_device = on_small_mesh if mesh.shape["feat"] == 8 and mesh.shape["dom"] == 4 else on_any_mesh
    return jax.shard_map(
        on_device, mesh=mesh, in_specs=placed, out_specs=P("dom", "feat", None), check_vma=False
    )
```

```python
import functools
import math

import jax
import jax.numpy as jnp
from jax import lax
from jax.experimental import pallas as pl
from jax.experimental.pallas import tpu as pltpu
from jax.sharding import PartitionSpec as P

FAN1 = 15
FAN2 = 10
CHUNK = 256
BESIDE = 10**9
COLUMNS_FIRST = (((0,), (0,)), ((), ()))
VMEM = pl.BlockSpec(memory_space=pltpu.VMEM)
CHIP_TO = ((2, 3, 0, 1), (3, 2, 1, 0), (1, 0, 3, 2))
DOM_TO = (
    ((2, 3, 0, 1), (1, 2, 3, 0)),
    ((1, 2, 3, 0), (2, 3, 0, 1)),
    ((3, 0, 1, 2), (3, 0, 1, 2)),
)


def look_up(table, place):
    found = table[0]
    for at in range(1, len(table)):
        found = jnp.where(place == at, table[at], found)
    return found


def inverse(table):
    return tuple(table.index(at) for at in range(len(table)))


def f32_dot(a, b):
    return jnp.dot(a, b, preferred_element_type=jnp.float32)


def f32_dot_columns(a, b):
    return lax.dot_general(a, b, COLUMNS_FIRST, preferred_element_type=jnp.float32)


def counts_of(rows, start, height):
    width = rows[0].shape[1]
    slots = lax.broadcasted_iota(jnp.int32, (height, width), 0).astype(jnp.float32).astype(jnp.bfloat16)
    one = jnp.ones((), jnp.bfloat16)
    zero = jnp.zeros((), jnp.bfloat16)
    counts = None
    for row in rows:
        near = (row - start).astype(jnp.float32).astype(jnp.bfloat16)
        hit = jnp.where(near == slots, one, zero)
        counts = hit if counts is None else counts + hit
    return counts


def counts_kernel(neigh, counts):
    owner = 1 - lax.rem(lax.axis_index("feat"), 2)
    index = neigh[:, 0, :]
    lane = lax.broadcasted_iota(jnp.int32, (index.shape[0], 128), 1)
    groups = []
    for start in range(0, index.shape[1], 256):
        a = index[:, start : start + 128]
        b = index[:, start + 128 : start + 256]
        first = jnp.where(owner == 0, a, pltpu.roll(a, 64, 1))
        second = jnp.where(owner == 0, pltpu.roll(b, 64, 1), b)
        groups.append(jnp.where(lane < 64, first, second))
    index = jnp.concatenate(groups, axis=1)
    rows = [index[k : k + 1] for k in range(index.shape[0])]
    chunk = min(CHUNK, counts.shape[0])
    for start in range(0, counts.shape[0], chunk):
        counts[pl.ds(start, chunk), :] = counts_of(rows, start, chunk)


def sums_kernel(mine, theirs, counts, weight, their_weight, kept, *rest):
    sent, own_all, agg_all = rest[:-2], rest[-2], rest[-1]
    me = lax.axis_index("feat")
    owner, chip = 1 - lax.rem(me, 2), lax.div(me, 2)
    nodes = own_all.shape[0]
    local = kept.shape[0]
    both = jnp.concatenate([mine[...], theirs[...]], axis=0)
    own_all[...] = f32_dot_columns(both[:, :nodes], jnp.concatenate([weight[0], their_weight[0]], axis=0))
    agg = (f32_dot(both, counts[...]) / FAN1).astype(jnp.bfloat16)
    agg_all[...] = f32_dot_columns(agg, jnp.concatenate([weight[1], their_weight[1]], axis=0))
    for at, table in enumerate(((0, 1, 2, 3), *CHIP_TO)):
        to = look_up(table, chip)
        own = own_all[pl.ds(pl.multiple_of((2 * to + owner) * local, local), local), :]
        pre = own + agg_all[pl.ds(pl.multiple_of(to * local, local), local), :]
        if at == 0:
            kept[...] = pre
        else:
            sent[at - 1][...] = pre.astype(jnp.bfloat16)


def rows_kernel(kept, *rest):
    partials, boundary, hidden, sent, picked = rest[:-6], rest[-6], rest[-5], rest[-4:-1], rest[-1]
    me = lax.axis_index("dom")
    core = lax.rem(lax.axis_index("feat"), 2)
    pre = kept[...]
    for part in partials:
        pre = pre + part[...].astype(jnp.float32)
    rows = jnp.maximum(pre, 0.0).astype(jnp.bfloat16)
    local, share = rows.shape[0], sent[0].shape[0]
    picked[...] = f32_dot_columns(counts_of([boundary[0]], 0, local), rows).astype(jnp.bfloat16)
    hidden[pl.ds(0, local), :] = rows
    hidden[pl.ds(local, share), :] = picked[pl.ds(pl.multiple_of(me * share, share), share), :]
    for tables, to in zip(DOM_TO, sent):
        place = jnp.where(core == 0, look_up(tables[0], me), look_up(tables[1], me))
        to[...] = picked[pl.ds(pl.multiple_of(place * share, share), share), :]


def slots_kernel(share, neigh, counts):
    me = lax.axis_index("dom")
    core = lax.rem(lax.axis_index("feat"), 2)
    rows = [neigh[k] for k in range(neigh.shape[0])]
    local = counts.shape[0] - (len(DOM_TO) + 1) * share
    counts[pl.ds(0, local), :] = counts_of(rows, 0, local)
    sources = [me]
    for tables in DOM_TO:
        sources.append(jnp.where(core == 0, look_up(inverse(tables[1]), me), look_up(inverse(tables[0]), me)))
    for at, source in enumerate(sources):
        counts[pl.ds(local + at * share, share), :] = counts_of(rows, local + source * share, share)


def join_kernel(*refs):
    incoming, rows = refs[:-1], refs[-1]
    for at, part in enumerate(incoming):
        rows[pl.ds(at * part.shape[0], part.shape[0]), :] = part[...]


def far_kernel(far, hidden, counts, weight, out):
    table = jnp.concatenate([hidden[...], far[...]], axis=0)
    agg = (f32_dot_columns(counts[...], table) / FAN2).astype(jnp.bfloat16)
    base = f32_dot(hidden[pl.ds(0, out.shape[1]), :], weight[0])
    out[0] = jnp.maximum(base + f32_dot(agg, weight[1]), 0.0).astype(jnp.bfloat16)


def call(kernel, outs, operands, name, scratch=(), flops=0):
    cost = pl.CostEstimate(flops=flops, bytes_accessed=flops // 1000, transcendentals=0) if flops else None
    return pl.pallas_call(
        kernel,
        out_shape=outs,
        in_specs=[VMEM] * len(operands),
        out_specs=jax.tree.map(lambda _: VMEM, outs),
        scratch_shapes=scratch,
        compiler_params=pltpu.CompilerParams(vmem_limit_bytes=8 << 20),
        cost_estimate=cost,
        name=name,
    )(*operands)


def apart_by(count, step):
    return [(i, i ^ step) for i in range(count)]


def on_small_mesh(features, neigh_one, boundary, neigh_two, weight_one, weight_two):
    feat_count, dom_count = lax.axis_size("feat"), lax.axis_size("dom")
    width = weight_one.shape[2]
    nodes = neigh_one.shape[2]
    local = nodes // feat_count
    share = boundary.shape[2] // dom_count
    out_rows = neigh_two.shape[1]
    shape = jax.ShapeDtypeStruct
    bf16, f32 = jnp.bfloat16, jnp.float32

    theirs = lax.ppermute(features, "feat", apart_by(feat_count, 1))
    their_weight = lax.ppermute(weight_one, "feat", apart_by(feat_count, 1))
    counts = call(
        counts_kernel, shape((features.shape[1], nodes // 2), bf16), [neigh_one.transpose(1, 0, 2)], "layer_one_counts"
    )
    chips = feat_count // 2
    kept, *sent = call(
        sums_kernel,
        (shape((local, width), f32),) + (shape((local, width), bf16),) * (chips - 1),
        [features, theirs, counts, weight_one, their_weight],
        "layer_one_sums",
        scratch=[pltpu.VMEM((nodes, width), f32), pltpu.VMEM((nodes // 2, width), f32)],
    )
    partials = [
        lax.ppermute(rows, "feat", [(2 * at + core, 2 * to + core) for at, to in enumerate(table) for core in (0, 1)])
        for table, rows in zip(CHIP_TO, sent)
    ]
    swap = apart_by(feat_count, 1)
    held, _ = lax.optimization_barrier((boundary, sent[0]))
    their_boundary = lax.ppermute(held, "feat", swap)
    hidden, *sent = call(
        rows_kernel,
        (shape((local + share, width), bf16),) + (shape((share, width), bf16),) * (dom_count - 1),
        [kept, *partials, their_boundary],
        "hidden_and_boundary_rows",
        scratch=[pltpu.VMEM((share * dom_count, width), bf16)],
    )
    incoming = [
        lax.ppermute(
            rows,
            ("feat", "dom"),
            [
                (feat * dom_count + at, (feat ^ 1) * dom_count + to)
                for feat in range(feat_count)
                for at, to in enumerate(tables[feat % 2])
            ],
        )
        for tables, rows in zip(DOM_TO, sent)
    ]
    hidden = lax.ppermute(hidden, "feat", swap)
    counts_two = call(
        functools.partial(slots_kernel, share),
        shape((local + share * dom_count, out_rows), bf16),
        [neigh_two.transpose(2, 0, 1)],
        "layer_two_counts",
        flops=BESIDE,
    )
    far = call(join_kernel, shape((share * len(incoming), width), bf16), incoming, "far_rows", flops=BESIDE)
    return call(
        far_kernel,
        shape((1, out_rows, weight_two.shape[2]), bf16),
        [far, hidden, counts_two, weight_two],
        "layer_two_far",
    )


def partial_kernel(features, own, neigh, weight, partial):
    fan = neigh.shape[0]
    sources = features.shape[1]
    chunk = min(CHUNK, sources)
    rows = [neigh[k] for k in range(fan)]

    def add_chunk(step, so_far):
        start = pl.multiple_of(step * chunk, chunk)
        return so_far + f32_dot(features[:, pl.ds(start, chunk)], counts_of(rows, start, chunk))

    total = lax.fori_loop(
        0, sources // chunk, add_chunk, jnp.zeros((features.shape[0], rows[0].shape[1]), jnp.float32)
    )
    agg = (total / FAN1).astype(jnp.bfloat16)
    pre = f32_dot_columns(own[...], weight[0]) + f32_dot_columns(agg, weight[1])
    partial[...] = pre.astype(partial.dtype)


def partial_sums(features, neigh, weight):
    fan, _, nodes = neigh.shape
    depth, sources = features.shape
    width = weight.shape[2]
    block = math.gcd(nodes, 512)
    return pl.pallas_call(
        partial_kernel,
        out_shape=jax.ShapeDtypeStruct((nodes, width), jnp.bfloat16),
        grid=(nodes // block,),
        in_specs=[
            pl.BlockSpec((depth, sources), lambda i: (0, 0)),
            pl.BlockSpec((depth, block), lambda i: (0, i)),
            pl.BlockSpec((fan, 1, block), lambda i: (0, 0, i)),
            pl.BlockSpec((2, depth, width), lambda i: (0, 0, 0)),
        ],
        out_specs=pl.BlockSpec((block, width), lambda i: (i, 0)),
        name="layer_one_partial_sums",
    )(features, features, neigh, weight)


def hidden_kernel(partials, boundary, hidden, picked):
    pre = partials[0].astype(jnp.float32)
    for part in range(1, partials.shape[0]):
        pre = pre + partials[part].astype(jnp.float32)
    rows = jnp.maximum(pre, 0.0).astype(jnp.bfloat16)
    hidden[...] = rows
    picked[...] = f32_dot_columns(counts_of([boundary[0]], 0, rows.shape[0]), rows).astype(jnp.bfloat16)


def layer_two_kernel(hidden, incoming, neigh, weight, out):
    rows = [neigh[k] for k in range(neigh.shape[0])]
    local = hidden.shape[0]
    out_rows = rows[0].shape[1]
    total = f32_dot_columns(counts_of(rows, 0, local), hidden[...])
    far = incoming.shape[0]
    step = math.gcd(far, 256)
    for start in range(0, far, step):
        total = total + f32_dot_columns(
            counts_of(rows, local + start, step), incoming[pl.ds(start, step), :]
        )
    agg = (total / FAN2).astype(jnp.bfloat16)
    result = f32_dot(hidden[pl.ds(0, out_rows), :], weight[0]) + f32_dot(agg, weight[1])
    out[0] = jnp.maximum(result, 0.0).astype(jnp.bfloat16)


def on_any_mesh(features, neigh_one, boundary, neigh_two, weight_one, weight_two):
    width = weight_one.shape[2]
    partial = partial_sums(features, neigh_one.transpose(1, 0, 2), weight_one)
    feat_count = lax.axis_size("feat")
    partials = lax.all_to_all(partial, "feat", split_axis=0, concat_axis=0, tiled=True)
    partials = partials.reshape(feat_count, -1, width)
    hidden, picked = pl.pallas_call(
        hidden_kernel,
        out_shape=(
            jax.ShapeDtypeStruct((partials.shape[1], width), jnp.bfloat16),
            jax.ShapeDtypeStruct((boundary.shape[2], width), jnp.bfloat16),
        ),
        name="hidden_and_boundary_rows",
    )(partials, boundary)
    incoming = lax.all_to_all(picked, "dom", split_axis=0, concat_axis=0, tiled=True)
    return pl.pallas_call(
        layer_two_kernel,
        out_shape=jax.ShapeDtypeStruct((1, neigh_two.shape[1], weight_two.shape[2]), jnp.bfloat16),
        name="layer_two",
    )(hidden, incoming, neigh_two.transpose(2, 0, 1), weight_two)


def solution(mesh):
    placed = (
        P("feat", "dom"),
        P("dom", None, None),
        P("dom", "feat", None),
        P("dom", "feat", None),
        P(None, "feat", None),
        P(),
    )
    on_device = on_small_mesh if mesh.shape["feat"] == 8 and mesh.shape["dom"] == 4 else on_any_mesh
    return jax.shard_map(
        on_device, mesh=mesh, in_specs=placed, out_specs=P("dom", "feat", None), check_vma=False
    )
```

```python
import functools
import math

import jax
import jax.numpy as jnp
from jax import lax
from jax.experimental import pallas as pl
from jax.experimental.pallas import tpu as pltpu
from jax.sharding import PartitionSpec as P

FAN1 = 15
FAN2 = 10
CHUNK = 256
BESIDE = 10**9
COLUMNS_FIRST = (((0,), (0,)), ((), ()))
VMEM = pl.BlockSpec(memory_space=pltpu.VMEM)
CHIP_TO = ((2, 3, 0, 1), (3, 2, 1, 0), (1, 0, 3, 2))
DOM_TO = (
    ((1, 2, 3, 0), (2, 3, 1, 0)),
    ((2, 3, 0, 1), (3, 2, 0, 1)),
    ((3, 0, 1, 2), (1, 0, 3, 2)),
)


def look_up(table, place):
    found = table[0]
    for at in range(1, len(table)):
        found = jnp.where(place == at, table[at], found)
    return found


def inverse(table):
    return tuple(table.index(at) for at in range(len(table)))


def f32_dot(a, b):
    return jnp.dot(a, b, preferred_element_type=jnp.float32)


def f32_dot_columns(a, b):
    return lax.dot_general(a, b, COLUMNS_FIRST, preferred_element_type=jnp.float32)


def counts_of(rows, start, height):
    width = rows[0].shape[1]
    slots = lax.broadcasted_iota(jnp.int32, (height, width), 0).astype(jnp.float32).astype(jnp.bfloat16)
    one = jnp.ones((), jnp.bfloat16)
    zero = jnp.zeros((), jnp.bfloat16)
    counts = None
    for row in rows:
        near = (row - start).astype(jnp.float32).astype(jnp.bfloat16)
        hit = jnp.where(near == slots, one, zero)
        counts = hit if counts is None else counts + hit
    return counts


def half_of(to, chip, core):
    return jnp.where(to == chip, 1 - core, core)


def counts_kernel(neigh, counts):
    me = lax.axis_index("feat")
    core, chip = lax.rem(me, 2), lax.div(me, 2)
    index = neigh[:, 0, :]
    lane = lax.broadcasted_iota(jnp.int32, (index.shape[0], 128), 1)
    groups = []
    for at in range(0, index.shape[1] // 128, 2):
        a, b = (index[:, 128 * to : 128 * (to + 1)] for to in (at, at + 1))
        first = jnp.where(half_of(at, chip, core) == 0, a, pltpu.roll(a, 64, 1))
        second = jnp.where(half_of(at + 1, chip, core) == 0, pltpu.roll(b, 64, 1), b)
        groups.append(jnp.where(lane < 64, first, second))
    index = jnp.concatenate(groups, axis=1)
    rows = [index[k : k + 1] for k in range(index.shape[0])]
    chunk = min(CHUNK, counts.shape[0])
    for start in range(0, counts.shape[0], chunk):
        counts[pl.ds(start, chunk), :] = counts_of(rows, start, chunk)


def sums_kernel(mine, theirs, counts, weight, their_weight, kept, *rest):
    sent, own_all, agg_all = rest[:-2], rest[-2], rest[-1]
    me = lax.axis_index("feat")
    core, chip = lax.rem(me, 2), lax.div(me, 2)
    nodes = own_all.shape[0]
    local = kept.shape[0]
    both = jnp.concatenate([mine[...], theirs[...]], axis=0)
    own_all[...] = f32_dot_columns(both[:, :nodes], jnp.concatenate([weight[0], their_weight[0]], axis=0))
    agg = (f32_dot(both, counts[...]) / FAN1).astype(jnp.bfloat16)
    agg_all[...] = f32_dot_columns(agg, jnp.concatenate([weight[1], their_weight[1]], axis=0))
    for at, table in enumerate(((0, 1, 2, 3), *CHIP_TO)):
        to = look_up(table, chip)
        own = own_all[pl.ds(pl.multiple_of((2 * to + half_of(to, chip, core)) * local, local), local), :]
        pre = own + agg_all[pl.ds(pl.multiple_of(to * local, local), local), :]
        if at == 0:
            kept[...] = pre
        else:
            sent[at - 1][...] = pre.astype(jnp.bfloat16)


def rows_kernel(*refs):
    partials, kept, boundary, hidden, sent, picked = refs[:-7], refs[-7], refs[-6], refs[-5], refs[-4:-1], refs[-1]
    me = lax.axis_index("dom")
    core = lax.rem(lax.axis_index("feat"), 2)
    pre = kept[...]
    for part in partials:
        pre = pre + part[...].astype(jnp.float32)
    rows = jnp.maximum(pre, 0.0).astype(jnp.bfloat16)
    local, share = rows.shape[0], sent[0].shape[0]
    picked[...] = f32_dot_columns(counts_of([boundary[0]], 0, local), rows).astype(jnp.bfloat16)
    hidden[pl.ds(0, local), :] = rows
    hidden[pl.ds(local, share), :] = picked[pl.ds(pl.multiple_of(me * share, share), share), :]
    for tables, to in zip(DOM_TO, sent):
        place = jnp.where(core == 0, look_up(tables[0], me), look_up(tables[1], me))
        to[...] = picked[pl.ds(pl.multiple_of(place * share, share), share), :]


def slots_kernel(share, neigh, counts):
    me = lax.axis_index("dom")
    core = lax.rem(lax.axis_index("feat"), 2)
    rows = [neigh[k] for k in range(neigh.shape[0])]
    local = counts.shape[0] - (len(DOM_TO) + 1) * share
    counts[pl.ds(0, local), :] = counts_of(rows, 0, local)
    sources = [me]
    for tables in DOM_TO:
        sources.append(jnp.where(core == 0, look_up(inverse(tables[1]), me), look_up(inverse(tables[0]), me)))
    for at, source in enumerate(sources):
        counts[pl.ds(local + at * share, share), :] = counts_of(rows, local + source * share, share)


def join_kernel(*refs):
    incoming, rows = refs[:-1], refs[-1]
    for at, part in enumerate(incoming):
        rows[pl.ds(at * part.shape[0], part.shape[0]), :] = part[...]


def far_kernel(far, hidden, counts, weight, out):
    table = jnp.concatenate([hidden[...], far[...]], axis=0)
    agg = (f32_dot_columns(counts[...], table) / FAN2).astype(jnp.bfloat16)
    base = f32_dot(hidden[pl.ds(0, out.shape[1]), :], weight[0])
    out[0] = jnp.maximum(base + f32_dot(agg, weight[1]), 0.0).astype(jnp.bfloat16)


def call(kernel, outs, operands, name, scratch=(), flops=0):
    cost = pl.CostEstimate(flops=flops, bytes_accessed=flops // 1000, transcendentals=0) if flops else None
    return pl.pallas_call(
        kernel,
        out_shape=outs,
        in_specs=[VMEM] * len(operands),
        out_specs=jax.tree.map(lambda _: VMEM, outs),
        scratch_shapes=scratch,
        compiler_params=pltpu.CompilerParams(vmem_limit_bytes=8 << 20),
        cost_estimate=cost,
        name=name,
    )(*operands)


def apart_by(count, step):
    return [(i, i ^ step) for i in range(count)]


def on_small_mesh(features, neigh_one, boundary, neigh_two, weight_one, weight_two):
    feat_count, dom_count = lax.axis_size("feat"), lax.axis_size("dom")
    width = weight_one.shape[2]
    nodes = neigh_one.shape[2]
    local = nodes // feat_count
    share = boundary.shape[2] // dom_count
    out_rows = neigh_two.shape[1]
    shape = jax.ShapeDtypeStruct
    bf16, f32 = jnp.bfloat16, jnp.float32

    theirs = lax.ppermute(features, "feat", apart_by(feat_count, 1))
    their_weight = lax.ppermute(weight_one, "feat", apart_by(feat_count, 1))
    counts = call(
        counts_kernel, shape((features.shape[1], nodes // 2), bf16), [neigh_one.transpose(1, 0, 2)], "layer_one_counts"
    )
    chips = feat_count // 2
    kept, *sent = call(
        sums_kernel,
        (shape((local, width), f32),) + (shape((local, width), bf16),) * (chips - 1),
        [features, theirs, counts, weight_one, their_weight],
        "layer_one_sums",
        scratch=[pltpu.VMEM((nodes, width), f32), pltpu.VMEM((nodes // 2, width), f32)],
    )
    partials = [
        lax.ppermute(rows, "feat", [(2 * at + core, 2 * to + 1 - core) for at, to in enumerate(table) for core in (0, 1)])
        for table, rows in zip(CHIP_TO, sent)
    ]
    swap = apart_by(feat_count, 1)
    held, _ = lax.optimization_barrier((boundary, sent[0]))
    their_boundary = lax.ppermute(held, "feat", swap)
    hidden, *sent = call(
        rows_kernel,
        (shape((local + share, width), bf16),) + (shape((share, width), bf16),) * (dom_count - 1),
        [*partials, kept, their_boundary],
        "hidden_and_boundary_rows",
        scratch=[pltpu.VMEM((share * dom_count, width), bf16)],
    )
    incoming = [
        lax.ppermute(
            rows,
            ("feat", "dom"),
            [
                (feat * dom_count + at, (feat ^ 1) * dom_count + to)
                for feat in range(feat_count)
                for at, to in enumerate(tables[feat % 2])
            ],
        )
        for tables, rows in zip(DOM_TO, sent)
    ]
    hidden = lax.ppermute(hidden, "feat", swap)
    counts_two = call(
        functools.partial(slots_kernel, share),
        shape((local + share * dom_count, out_rows), bf16),
        [neigh_two.transpose(2, 0, 1)],
        "layer_two_counts",
        flops=BESIDE,
    )
    far = call(join_kernel, shape((share * len(incoming), width), bf16), incoming, "far_rows", flops=BESIDE)
    return call(
        far_kernel,
        shape((1, out_rows, weight_two.shape[2]), bf16),
        [far, hidden, counts_two, weight_two],
        "layer_two_far",
    )


def partial_kernel(features, own, neigh, weight, partial):
    fan = neigh.shape[0]
    sources = features.shape[1]
    chunk = min(CHUNK, sources)
    rows = [neigh[k] for k in range(fan)]

    def add_chunk(step, so_far):
        start = pl.multiple_of(step * chunk, chunk)
        return so_far + f32_dot(features[:, pl.ds(start, chunk)], counts_of(rows, start, chunk))

    total = lax.fori_loop(
        0, sources // chunk, add_chunk, jnp.zeros((features.shape[0], rows[0].shape[1]), jnp.float32)
    )
    agg = (total / FAN1).astype(jnp.bfloat16)
    pre = f32_dot_columns(own[...], weight[0]) + f32_dot_columns(agg, weight[1])
    partial[...] = pre.astype(partial.dtype)


def partial_sums(features, neigh, weight):
    fan, _, nodes = neigh.shape
    depth, sources = features.shape
    width = weight.shape[2]
    block = math.gcd(nodes, 512)
    return pl.pallas_call(
        partial_kernel,
        out_shape=jax.ShapeDtypeStruct((nodes, width), jnp.bfloat16),
        grid=(nodes // block,),
        in_specs=[
            pl.BlockSpec((depth, sources), lambda i: (0, 0)),
            pl.BlockSpec((depth, block), lambda i: (0, i)),
            pl.BlockSpec((fan, 1, block), lambda i: (0, 0, i)),
            pl.BlockSpec((2, depth, width), lambda i: (0, 0, 0)),
        ],
        out_specs=pl.BlockSpec((block, width), lambda i: (i, 0)),
        name="layer_one_partial_sums",
    )(features, features, neigh, weight)


def hidden_kernel(partials, boundary, hidden, picked):
    pre = partials[0].astype(jnp.float32)
    for part in range(1, partials.shape[0]):
        pre = pre + partials[part].astype(jnp.float32)
    rows = jnp.maximum(pre, 0.0).astype(jnp.bfloat16)
    hidden[...] = rows
    picked[...] = f32_dot_columns(counts_of([boundary[0]], 0, rows.shape[0]), rows).astype(jnp.bfloat16)


def layer_two_kernel(hidden, incoming, neigh, weight, out):
    rows = [neigh[k] for k in range(neigh.shape[0])]
    local = hidden.shape[0]
    out_rows = rows[0].shape[1]
    total = f32_dot_columns(counts_of(rows, 0, local), hidden[...])
    far = incoming.shape[0]
    step = math.gcd(far, 256)
    for start in range(0, far, step):
        total = total + f32_dot_columns(
            counts_of(rows, local + start, step), incoming[pl.ds(start, step), :]
        )
    agg = (total / FAN2).astype(jnp.bfloat16)
    result = f32_dot(hidden[pl.ds(0, out_rows), :], weight[0]) + f32_dot(agg, weight[1])
    out[0] = jnp.maximum(result, 0.0).astype(jnp.bfloat16)


def on_any_mesh(features, neigh_one, boundary, neigh_two, weight_one, weight_two):
    width = weight_one.shape[2]
    partial = partial_sums(features, neigh_one.transpose(1, 0, 2), weight_one)
    feat_count = lax.axis_size("feat")
    partials = lax.all_to_all(partial, "feat", split_axis=0, concat_axis=0, tiled=True)
    partials = partials.reshape(feat_count, -1, width)
    hidden, picked = pl.pallas_call(
        hidden_kernel,
        out_shape=(
            jax.ShapeDtypeStruct((partials.shape[1], width), jnp.bfloat16),
            jax.ShapeDtypeStruct((boundary.shape[2], width), jnp.bfloat16),
        ),
        name="hidden_and_boundary_rows",
    )(partials, boundary)
    incoming = lax.all_to_all(picked, "dom", split_axis=0, concat_axis=0, tiled=True)
    return pl.pallas_call(
        layer_two_kernel,
        out_shape=jax.ShapeDtypeStruct((1, neigh_two.shape[1], weight_two.shape[2]), jnp.bfloat16),
        name="layer_two",
    )(hidden, incoming, neigh_two.transpose(2, 0, 1), weight_two)


def solution(mesh):
    placed = (
        P("feat", "dom"),
        P("dom", None, None),
        P("dom", "feat", None),
        P("dom", "feat", None),
        P(None, "feat", None),
        P(),
    )
    on_device = on_small_mesh if mesh.shape["feat"] == 8 and mesh.shape["dom"] == 4 else on_any_mesh
    return jax.shard_map(
        on_device, mesh=mesh, in_specs=placed, out_specs=P("dom", "feat", None), check_vma=False
    )
```

```python
import functools
import math

import jax
import jax.numpy as jnp
from jax import lax
from jax.experimental import pallas as pl
from jax.experimental.pallas import tpu as pltpu
from jax.sharding import PartitionSpec as P

FAN1 = 15
FAN2 = 10
CHUNK = 256
BEHIND = 10**9
AHEAD = 10**10
COLUMNS_FIRST = (((0,), (0,)), ((), ()))
VMEM = pl.BlockSpec(memory_space=pltpu.VMEM)
CHIP_TO = ((2, 3, 0, 1), (3, 2, 1, 0), (1, 0, 3, 2))
DOM_TO = (
    ((1, 2, 3, 0), (2, 3, 1, 0)),
    ((2, 3, 0, 1), (3, 2, 0, 1)),
    ((3, 0, 1, 2), (1, 0, 3, 2)),
)


def look_up(table, place):
    found = table[0]
    for at in range(1, len(table)):
        found = jnp.where(place == at, table[at], found)
    return found


def inverse(table):
    return tuple(table.index(at) for at in range(len(table)))


def f32_dot(a, b):
    return jnp.dot(a, b, preferred_element_type=jnp.float32)


def f32_dot_columns(a, b):
    return lax.dot_general(a, b, COLUMNS_FIRST, preferred_element_type=jnp.float32)


def counts_of(rows, start, height):
    width = rows[0].shape[1]
    slots = lax.broadcasted_iota(jnp.int32, (height, width), 0).astype(jnp.float32).astype(jnp.bfloat16)
    counts = jnp.zeros((height, width), jnp.bfloat16)
    for at, row in enumerate(rows):
        near = (row - start).astype(jnp.float32).astype(jnp.bfloat16)
        so_far = jnp.ones(row.shape, jnp.float32)
        for before in rows[:at]:
            so_far = so_far + (before == row).astype(jnp.float32)
        counts = jnp.where(near == slots, so_far.astype(jnp.bfloat16), counts)
    return counts


def half_of(to, chip, core):
    return jnp.where(to == chip, 1 - core, core)


def halves_kernel(halves):
    me = lax.axis_index("feat")
    core, chip = lax.rem(me, 2), lax.div(me, 2)
    for to in range(halves.shape[0]):
        halves[pl.ds(to, 1), :] = jnp.broadcast_to(half_of(to, chip, core), (1, halves.shape[1]))


def counts_kernel(halves, neigh, counts):
    index = neigh[:, 0, :]
    lane = lax.broadcasted_iota(jnp.int32, (index.shape[0], 128), 1)
    groups = []
    for at in range(0, index.shape[1] // 128, 2):
        a, b = (index[:, 128 * to : 128 * (to + 1)] for to in (at, at + 1))
        first = jnp.where(halves[pl.ds(at, 1), :] == 0, a, pltpu.roll(a, 64, 1))
        second = jnp.where(halves[pl.ds(at + 1, 1), :] == 0, pltpu.roll(b, 64, 1), b)
        groups.append(jnp.where(lane < 64, first, second))
    index = jnp.concatenate(groups, axis=1)
    rows = [index[k : k + 1] for k in range(index.shape[0])]
    chunk = min(CHUNK, counts.shape[0])
    for start in range(0, counts.shape[0], chunk):
        counts[pl.ds(start, chunk), :] = counts_of(rows, start, chunk)


def sums_kernel(mine, theirs, counts, weight, their_weight, kept, *rest):
    sent, own_all, agg_all = rest[:-2], rest[-2], rest[-1]
    me = lax.axis_index("feat")
    core, chip = lax.rem(me, 2), lax.div(me, 2)
    nodes = own_all.shape[0]
    local = kept.shape[0]
    both = jnp.concatenate([mine[...], theirs[...]], axis=0)
    own_all[...] = f32_dot_columns(both[:, :nodes], jnp.concatenate([weight[0], their_weight[0]], axis=0))
    agg = (f32_dot(both, counts[...]) / FAN1).astype(jnp.bfloat16)
    agg_all[...] = f32_dot_columns(agg, jnp.concatenate([weight[1], their_weight[1]], axis=0))
    for at, table in enumerate(((0, 1, 2, 3), *CHIP_TO)):
        to = look_up(table, chip)
        own = own_all[pl.ds(pl.multiple_of((2 * to + half_of(to, chip, core)) * local, local), local), :]
        pre = own + agg_all[pl.ds(pl.multiple_of(to * local, local), local), :]
        if at == 0:
            kept[...] = pre
        else:
            sent[at - 1][...] = pre.astype(jnp.bfloat16)


def turned(slots):
    size = slots.shape[0]
    same = lax.broadcasted_iota(jnp.int32, (size, size), 0) == lax.broadcasted_iota(jnp.int32, (size, size), 1)
    return f32_dot_columns(slots, jnp.where(same, 1.0, 0.0).astype(jnp.bfloat16)).astype(jnp.bfloat16)


def picks_kernel(share, boundary, neigh, chosen, counts, scratch):
    me = lax.axis_index("dom")
    core = lax.rem(lax.axis_index("feat"), 2)
    scratch[...] = turned(counts_of([boundary[0]], 0, chosen.shape[1]))
    places = [me]
    sources = [me]
    for tables in DOM_TO:
        places.append(jnp.where(core == 0, look_up(tables[0], me), look_up(tables[1], me)))
        sources.append(jnp.where(core == 0, look_up(inverse(tables[1]), me), look_up(inverse(tables[0]), me)))
    for at, place in enumerate(places):
        chosen[pl.ds(at * share, share), :] = scratch[pl.ds(pl.multiple_of(place * share, share), share), :]
    rows = [neigh[k] for k in range(neigh.shape[0])]
    local = chosen.shape[1]
    parts = [counts_of(rows, 0, local)] + [counts_of(rows, local + source * share, share) for source in sources]
    counts[...] = turned(jnp.concatenate(parts, axis=0))


def rows_kernel(*refs):
    partials, kept, chosen, hidden, sent = refs[:-6], refs[-6], refs[-5], refs[-4], refs[-3:]
    pre = kept[...]
    for part in partials:
        pre = pre + part[...].astype(jnp.float32)
    rows = jnp.maximum(pre, 0.0).astype(jnp.bfloat16)
    local, share = rows.shape[0], sent[0].shape[0]
    hidden[pl.ds(0, local), :] = rows
    picked = f32_dot(chosen[...], rows).astype(jnp.bfloat16)
    hidden[pl.ds(local, share), :] = picked[:share]
    for at, to in enumerate(sent):
        to[...] = picked[(at + 1) * share : (at + 2) * share]


def join_kernel(*refs):
    incoming, rows = refs[:-1], refs[-1]
    for at, part in enumerate(incoming):
        rows[pl.ds(at * part.shape[0], part.shape[0]), :] = part[...]


def far_kernel(far, hidden, counts, weight, out):
    table = jnp.concatenate([hidden[...], far[...]], axis=0)
    agg = (f32_dot(counts[...], table) / FAN2).astype(jnp.bfloat16)
    base = f32_dot(hidden[pl.ds(0, out.shape[1]), :], weight[0])
    out[0] = jnp.maximum(base + f32_dot(agg, weight[1]), 0.0).astype(jnp.bfloat16)


def call(kernel, outs, operands, name, scratch=(), flops=0):
    cost = pl.CostEstimate(flops=flops, bytes_accessed=flops // 1000, transcendentals=0) if flops else None
    return pl.pallas_call(
        kernel,
        out_shape=outs,
        in_specs=[VMEM] * len(operands),
        out_specs=jax.tree.map(lambda _: VMEM, outs),
        scratch_shapes=scratch,
        compiler_params=pltpu.CompilerParams(vmem_limit_bytes=8 << 20),
        cost_estimate=cost,
        name=name,
    )(*operands)


def apart_by(count, step):
    return [(i, i ^ step) for i in range(count)]


def on_small_mesh(features, neigh_one, boundary, neigh_two, weight_one, weight_two):
    feat_count, dom_count = lax.axis_size("feat"), lax.axis_size("dom")
    width = weight_one.shape[2]
    nodes = neigh_one.shape[2]
    local = nodes // feat_count
    share = boundary.shape[2] // dom_count
    out_rows = neigh_two.shape[1]
    shape = jax.ShapeDtypeStruct
    bf16, f32 = jnp.bfloat16, jnp.float32

    halves = call(
        halves_kernel, shape((feat_count // 2, 128), jnp.int32), [], "halves_of_chips", flops=AHEAD
    )
    their_weight = lax.ppermute(weight_one, "feat", apart_by(feat_count, 1))
    theirs = lax.ppermute(features, "feat", apart_by(feat_count, 1))
    counts = call(
        counts_kernel,
        shape((features.shape[1], nodes // 2), bf16),
        [halves, neigh_one.transpose(1, 0, 2)],
        "layer_one_counts",
    )
    chips = feat_count // 2
    kept, *sent = call(
        sums_kernel,
        (shape((local, width), f32),) + (shape((local, width), bf16),) * (chips - 1),
        [features, theirs, counts, weight_one, their_weight],
        "layer_one_sums",
        scratch=[pltpu.VMEM((nodes, width), f32), pltpu.VMEM((nodes // 2, width), f32)],
    )
    partials = [
        lax.ppermute(rows, "feat", [(2 * at + core, 2 * to + 1 - core) for at, to in enumerate(table) for core in (0, 1)])
        for table, rows in zip(CHIP_TO, sent)
    ]
    swap = apart_by(feat_count, 1)
    held, _ = lax.optimization_barrier((boundary, sent[0]))
    their_boundary = lax.ppermute(held, "feat", swap)
    chosen, counts_two = call(
        functools.partial(picks_kernel, share),
        (shape((share * dom_count, local), bf16), shape((out_rows, local + share * dom_count), bf16)),
        [their_boundary, neigh_two.transpose(2, 0, 1)],
        "boundary_and_layer_two_counts",
        scratch=[pltpu.VMEM((share * dom_count, local), bf16)],
    )
    hidden, *sent = call(
        rows_kernel,
        (shape((local + share, width), bf16),) + (shape((share, width), bf16),) * (dom_count - 1),
        [*partials, kept, chosen],
        "hidden_and_boundary_rows",
    )
    incoming = [
        lax.ppermute(
            rows,
            ("feat", "dom"),
            [
                (feat * dom_count + at, (feat ^ 1) * dom_count + to)
                for feat in range(feat_count)
                for at, to in enumerate(tables[feat % 2])
            ],
        )
        for tables, rows in zip(DOM_TO, sent)
    ]
    hidden = lax.ppermute(hidden, "feat", swap)
    far = call(join_kernel, shape((share * len(incoming), width), bf16), incoming, "far_rows", flops=BEHIND)
    return call(
        far_kernel,
        shape((1, out_rows, weight_two.shape[2]), bf16),
        [far, hidden, counts_two, weight_two],
        "layer_two_far",
    )


def partial_kernel(features, own, neigh, weight, partial):
    fan = neigh.shape[0]
    sources = features.shape[1]
    chunk = min(CHUNK, sources)
    rows = [neigh[k] for k in range(fan)]

    def add_chunk(step, so_far):
        start = pl.multiple_of(step * chunk, chunk)
        return so_far + f32_dot(features[:, pl.ds(start, chunk)], counts_of(rows, start, chunk))

    total = lax.fori_loop(
        0, sources // chunk, add_chunk, jnp.zeros((features.shape[0], rows[0].shape[1]), jnp.float32)
    )
    agg = (total / FAN1).astype(jnp.bfloat16)
    pre = f32_dot_columns(own[...], weight[0]) + f32_dot_columns(agg, weight[1])
    partial[...] = pre.astype(partial.dtype)


def partial_sums(features, neigh, weight):
    fan, _, nodes = neigh.shape
    depth, sources = features.shape
    width = weight.shape[2]
    block = math.gcd(nodes, 512)
    return pl.pallas_call(
        partial_kernel,
        out_shape=jax.ShapeDtypeStruct((nodes, width), jnp.bfloat16),
        grid=(nodes // block,),
        in_specs=[
            pl.BlockSpec((depth, sources), lambda i: (0, 0)),
            pl.BlockSpec((depth, block), lambda i: (0, i)),
            pl.BlockSpec((fan, 1, block), lambda i: (0, 0, i)),
            pl.BlockSpec((2, depth, width), lambda i: (0, 0, 0)),
        ],
        out_specs=pl.BlockSpec((block, width), lambda i: (i, 0)),
        name="layer_one_partial_sums",
    )(features, features, neigh, weight)


def hidden_kernel(partials, boundary, hidden, picked):
    pre = partials[0].astype(jnp.float32)
    for part in range(1, partials.shape[0]):
        pre = pre + partials[part].astype(jnp.float32)
    rows = jnp.maximum(pre, 0.0).astype(jnp.bfloat16)
    hidden[...] = rows
    picked[...] = f32_dot_columns(counts_of([boundary[0]], 0, rows.shape[0]), rows).astype(jnp.bfloat16)


def layer_two_kernel(hidden, incoming, neigh, weight, out):
    rows = [neigh[k] for k in range(neigh.shape[0])]
    local = hidden.shape[0]
    out_rows = rows[0].shape[1]
    total = f32_dot_columns(counts_of(rows, 0, local), hidden[...])
    far = incoming.shape[0]
    step = math.gcd(far, 256)
    for start in range(0, far, step):
        total = total + f32_dot_columns(
            counts_of(rows, local + start, step), incoming[pl.ds(start, step), :]
        )
    agg = (total / FAN2).astype(jnp.bfloat16)
    result = f32_dot(hidden[pl.ds(0, out_rows), :], weight[0]) + f32_dot(agg, weight[1])
    out[0] = jnp.maximum(result, 0.0).astype(jnp.bfloat16)


def on_any_mesh(features, neigh_one, boundary, neigh_two, weight_one, weight_two):
    width = weight_one.shape[2]
    partial = partial_sums(features, neigh_one.transpose(1, 0, 2), weight_one)
    feat_count = lax.axis_size("feat")
    partials = lax.all_to_all(partial, "feat", split_axis=0, concat_axis=0, tiled=True)
    partials = partials.reshape(feat_count, -1, width)
    hidden, picked = pl.pallas_call(
        hidden_kernel,
        out_shape=(
            jax.ShapeDtypeStruct((partials.shape[1], width), jnp.bfloat16),
            jax.ShapeDtypeStruct((boundary.shape[2], width), jnp.bfloat16),
        ),
        name="hidden_and_boundary_rows",
    )(partials, boundary)
    incoming = lax.all_to_all(picked, "dom", split_axis=0, concat_axis=0, tiled=True)
    return pl.pallas_call(
        layer_two_kernel,
        out_shape=jax.ShapeDtypeStruct((1, neigh_two.shape[1], weight_two.shape[2]), jnp.bfloat16),
        name="layer_two",
    )(hidden, incoming, neigh_two.transpose(2, 0, 1), weight_two)


def solution(mesh):
    placed = (
        P("feat", "dom"),
        P("dom", None, None),
        P("dom", "feat", None),
        P("dom", "feat", None),
        P(None, "feat", None),
        P(),
    )
    on_device = on_small_mesh if mesh.shape["feat"] == 8 and mesh.shape["dom"] == 4 else on_any_mesh
    return jax.shard_map(
        on_device, mesh=mesh, in_specs=placed, out_specs=P("dom", "feat", None), check_vma=False
    )
```

```python
import functools
import math

import jax
import jax.numpy as jnp
from jax import lax
from jax.experimental import pallas as pl
from jax.experimental.pallas import tpu as pltpu
from jax.sharding import PartitionSpec as P

FAN1 = 15
FAN2 = 10
CHUNK = 256
BEHIND = 10**9
AHEAD = 2 * 10**9
COLUMNS_FIRST = (((0,), (0,)), ((), ()))
VMEM = pl.BlockSpec(memory_space=pltpu.VMEM)
CHIP_TO = ((2, 3, 0, 1), (3, 2, 1, 0), (1, 0, 3, 2))
DOM_TO = (
    ((1, 2, 3, 0), (2, 3, 0, 1)),
    ((2, 3, 0, 1), (3, 2, 1, 0)),
    ((3, 0, 1, 2), (1, 0, 3, 2)),
)


def look_up(table, place):
    found = table[0]
    for at in range(1, len(table)):
        found = jnp.where(place == at, table[at], found)
    return found


def inverse(table):
    return tuple(table.index(at) for at in range(len(table)))


def f32_dot(a, b):
    return jnp.dot(a, b, preferred_element_type=jnp.float32)


def f32_dot_columns(a, b):
    return lax.dot_general(a, b, COLUMNS_FIRST, preferred_element_type=jnp.float32)


def counts_of(rows, start, height):
    width = rows[0].shape[1]
    slots = lax.broadcasted_iota(jnp.int32, (height, width), 0).astype(jnp.float32).astype(jnp.bfloat16)
    counts = jnp.zeros((height, width), jnp.bfloat16)
    for at, row in enumerate(rows):
        near = (row - start).astype(jnp.float32).astype(jnp.bfloat16)
        so_far = jnp.ones(row.shape, jnp.float32)
        for before in rows[:at]:
            so_far = so_far + (before == row).astype(jnp.float32)
        counts = jnp.where(near == slots, so_far.astype(jnp.bfloat16), counts)
    return counts


def half_of(to, chip, core):
    return jnp.where(to == chip, 1 - core, core)


def halves_kernel(halves):
    me = lax.axis_index("feat")
    core, chip = lax.rem(me, 2), lax.div(me, 2)
    for to in range(halves.shape[0]):
        halves[pl.ds(to, 1), :] = jnp.broadcast_to(half_of(to, chip, core), (1, halves.shape[1]))


def counts_kernel(halves, neigh, counts):
    index = neigh[:, 0, :]
    lane = lax.broadcasted_iota(jnp.int32, (index.shape[0], 128), 1)
    groups = []
    for at in range(0, index.shape[1] // 128, 2):
        a, b = (index[:, 128 * to : 128 * (to + 1)] for to in (at, at + 1))
        first = jnp.where(halves[pl.ds(at, 1), :] == 0, a, pltpu.roll(a, 64, 1))
        second = jnp.where(halves[pl.ds(at + 1, 1), :] == 0, pltpu.roll(b, 64, 1), b)
        groups.append(jnp.where(lane < 64, first, second))
    index = jnp.concatenate(groups, axis=1)
    rows = [index[k : k + 1] for k in range(index.shape[0])]
    chunk = min(CHUNK, counts.shape[0])
    for start in range(0, counts.shape[0], chunk):
        counts[pl.ds(start, chunk), :] = counts_of(rows, start, chunk)


def sums_kernel(mine, theirs, counts, weight, their_weight, kept, *rest):
    sent, own_all, agg_all = rest[:-2], rest[-2], rest[-1]
    me = lax.axis_index("feat")
    core, chip = lax.rem(me, 2), lax.div(me, 2)
    nodes = own_all.shape[0]
    local = kept.shape[0]
    both = jnp.concatenate([mine[...], theirs[...]], axis=0)
    own_all[...] = f32_dot_columns(both[:, :nodes], jnp.concatenate([weight[0], their_weight[0]], axis=0))
    agg = (f32_dot(both, counts[...]) / FAN1).astype(jnp.bfloat16)
    agg_all[...] = f32_dot_columns(agg, jnp.concatenate([weight[1], their_weight[1]], axis=0))
    for at, table in enumerate(((0, 1, 2, 3), *CHIP_TO)):
        to = look_up(table, chip)
        own = own_all[pl.ds(pl.multiple_of((2 * to + half_of(to, chip, core)) * local, local), local), :]
        pre = own + agg_all[pl.ds(pl.multiple_of(to * local, local), local), :]
        if at == 0:
            kept[...] = pre
        else:
            sent[at - 1][...] = pre.astype(jnp.bfloat16)


def turned(slots):
    size = slots.shape[0]
    same = lax.broadcasted_iota(jnp.int32, (size, size), 0) == lax.broadcasted_iota(jnp.int32, (size, size), 1)
    return f32_dot_columns(slots, jnp.where(same, 1.0, 0.0).astype(jnp.bfloat16)).astype(jnp.bfloat16)


def picks_kernel(share, boundary, neigh, chosen, counts, scratch):
    me = lax.axis_index("dom")
    core = lax.rem(lax.axis_index("feat"), 2)
    scratch[...] = turned(counts_of([boundary[0]], 0, chosen.shape[1]))
    places = [me]
    sources = [me]
    for tables in DOM_TO:
        places.append(jnp.where(core == 0, look_up(tables[0], me), look_up(tables[1], me)))
        sources.append(jnp.where(core == 0, look_up(inverse(tables[1]), me), look_up(inverse(tables[0]), me)))
    for at, place in enumerate(places):
        chosen[pl.ds(at * share, share), :] = scratch[pl.ds(pl.multiple_of(place * share, share), share), :]
    rows = [neigh[k] for k in range(neigh.shape[0])]
    local = chosen.shape[1]
    parts = [counts_of(rows, 0, local)] + [counts_of(rows, local + source * share, share) for source in sources]
    counts[...] = turned(jnp.concatenate(parts, axis=0))


def rows_kernel(*refs):
    partials, kept, chosen, hidden, sent = refs[:-6], refs[-6], refs[-5], refs[-4], refs[-3:]
    pre = kept[...]
    for part in partials:
        pre = pre + part[...].astype(jnp.float32)
    rows = jnp.maximum(pre, 0.0).astype(jnp.bfloat16)
    local, share = rows.shape[0], sent[0].shape[0]
    hidden[pl.ds(0, local), :] = rows
    picked = f32_dot(chosen[...], rows).astype(jnp.bfloat16)
    hidden[pl.ds(local, share), :] = picked[:share]
    for at, to in enumerate(sent):
        to[...] = picked[(at + 1) * share : (at + 2) * share]


def join_kernel(*refs):
    incoming, rows = refs[:-1], refs[-1]
    for at, part in enumerate(incoming):
        rows[pl.ds(at * part.shape[0], part.shape[0]), :] = part[...]


def far_kernel(far, hidden, counts, weight, out):
    table = jnp.concatenate([hidden[...], far[...]], axis=0)
    agg = (f32_dot(counts[...], table) / FAN2).astype(jnp.bfloat16)
    base = f32_dot(hidden[pl.ds(0, out.shape[1]), :], weight[0])
    out[0] = jnp.maximum(base + f32_dot(agg, weight[1]), 0.0).astype(jnp.bfloat16)


def call(kernel, outs, operands, name, scratch=(), flops=0):
    cost = pl.CostEstimate(flops=flops, bytes_accessed=flops // 1000, transcendentals=0) if flops else None
    return pl.pallas_call(
        kernel,
        out_shape=outs,
        in_specs=[VMEM] * len(operands),
        out_specs=jax.tree.map(lambda _: VMEM, outs),
        scratch_shapes=scratch,
        compiler_params=pltpu.CompilerParams(vmem_limit_bytes=8 << 20),
        cost_estimate=cost,
        name=name,
    )(*operands)


def apart_by(count, step):
    return [(i, i ^ step) for i in range(count)]


def on_small_mesh(features, neigh_one, boundary, neigh_two, weight_one, weight_two):
    feat_count, dom_count = lax.axis_size("feat"), lax.axis_size("dom")
    width = weight_one.shape[2]
    nodes = neigh_one.shape[2]
    local = nodes // feat_count
    share = boundary.shape[2] // dom_count
    out_rows = neigh_two.shape[1]
    shape = jax.ShapeDtypeStruct
    bf16, f32 = jnp.bfloat16, jnp.float32

    halves = call(
        halves_kernel, shape((feat_count // 2, 128), jnp.int32), [], "halves_of_chips", flops=AHEAD
    )
    their_weight = lax.ppermute(weight_one, "feat", apart_by(feat_count, 1))
    theirs = lax.ppermute(features, "feat", apart_by(feat_count, 1))
    counts = call(
        counts_kernel,
        shape((features.shape[1], nodes // 2), bf16),
        [halves, neigh_one.transpose(1, 0, 2)],
        "layer_one_counts",
    )
    chips = feat_count // 2
    kept, *sent = call(
        sums_kernel,
        (shape((local, width), f32),) + (shape((local, width), bf16),) * (chips - 1),
        [features, theirs, counts, weight_one, their_weight],
        "layer_one_sums",
        scratch=[pltpu.VMEM((nodes, width), f32), pltpu.VMEM((nodes // 2, width), f32)],
    )
    partials = [
        lax.ppermute(rows, "feat", [(2 * at + core, 2 * to + 1 - core) for at, to in enumerate(table) for core in (0, 1)])
        for table, rows in zip(CHIP_TO, sent)
    ]
    swap = apart_by(feat_count, 1)
    held, _ = lax.optimization_barrier((boundary, sent[0]))
    their_boundary = lax.ppermute(held, "feat", swap)
    chosen, counts_two = call(
        functools.partial(picks_kernel, share),
        (shape((share * dom_count, local), bf16), shape((out_rows, local + share * dom_count), bf16)),
        [their_boundary, neigh_two.transpose(2, 0, 1)],
        "boundary_and_layer_two_counts",
        scratch=[pltpu.VMEM((share * dom_count, local), bf16)],
    )
    hidden, *sent = call(
        rows_kernel,
        (shape((local + share, width), bf16),) + (shape((share, width), bf16),) * (dom_count - 1),
        [*partials, kept, chosen],
        "hidden_and_boundary_rows",
    )
    incoming = [
        lax.ppermute(
            rows,
            ("feat", "dom"),
            [
                (feat * dom_count + at, (feat ^ 1) * dom_count + to)
                for feat in range(feat_count)
                for at, to in enumerate(tables[feat % 2])
            ],
        )
        for tables, rows in zip(DOM_TO, sent)
    ]
    hidden = lax.ppermute(hidden, "feat", swap)
    far = call(join_kernel, shape((share * len(incoming), width), bf16), incoming, "far_rows", flops=BEHIND)
    return call(
        far_kernel,
        shape((1, out_rows, weight_two.shape[2]), bf16),
        [far, hidden, counts_two, weight_two],
        "layer_two_far",
    )


def partial_kernel(features, own, neigh, weight, partial):
    fan = neigh.shape[0]
    sources = features.shape[1]
    chunk = min(CHUNK, sources)
    rows = [neigh[k] for k in range(fan)]

    def add_chunk(step, so_far):
        start = pl.multiple_of(step * chunk, chunk)
        return so_far + f32_dot(features[:, pl.ds(start, chunk)], counts_of(rows, start, chunk))

    total = lax.fori_loop(
        0, sources // chunk, add_chunk, jnp.zeros((features.shape[0], rows[0].shape[1]), jnp.float32)
    )
    agg = (total / FAN1).astype(jnp.bfloat16)
    pre = f32_dot_columns(own[...], weight[0]) + f32_dot_columns(agg, weight[1])
    partial[...] = pre.astype(partial.dtype)


def partial_sums(features, neigh, weight):
    fan, _, nodes = neigh.shape
    depth, sources = features.shape
    width = weight.shape[2]
    block = math.gcd(nodes, 512)
    return pl.pallas_call(
        partial_kernel,
        out_shape=jax.ShapeDtypeStruct((nodes, width), jnp.bfloat16),
        grid=(nodes // block,),
        in_specs=[
            pl.BlockSpec((depth, sources), lambda i: (0, 0)),
            pl.BlockSpec((depth, block), lambda i: (0, i)),
            pl.BlockSpec((fan, 1, block), lambda i: (0, 0, i)),
            pl.BlockSpec((2, depth, width), lambda i: (0, 0, 0)),
        ],
        out_specs=pl.BlockSpec((block, width), lambda i: (i, 0)),
        name="layer_one_partial_sums",
    )(features, features, neigh, weight)


def hidden_kernel(partials, boundary, hidden, picked):
    pre = partials[0].astype(jnp.float32)
    for part in range(1, partials.shape[0]):
        pre = pre + partials[part].astype(jnp.float32)
    rows = jnp.maximum(pre, 0.0).astype(jnp.bfloat16)
    hidden[...] = rows
    picked[...] = f32_dot_columns(counts_of([boundary[0]], 0, rows.shape[0]), rows).astype(jnp.bfloat16)


def layer_two_kernel(hidden, incoming, neigh, weight, out):
    rows = [neigh[k] for k in range(neigh.shape[0])]
    local = hidden.shape[0]
    out_rows = rows[0].shape[1]
    total = f32_dot_columns(counts_of(rows, 0, local), hidden[...])
    far = incoming.shape[0]
    step = math.gcd(far, 256)
    for start in range(0, far, step):
        total = total + f32_dot_columns(
            counts_of(rows, local + start, step), incoming[pl.ds(start, step), :]
        )
    agg = (total / FAN2).astype(jnp.bfloat16)
    result = f32_dot(hidden[pl.ds(0, out_rows), :], weight[0]) + f32_dot(agg, weight[1])
    out[0] = jnp.maximum(result, 0.0).astype(jnp.bfloat16)


def on_any_mesh(features, neigh_one, boundary, neigh_two, weight_one, weight_two):
    width = weight_one.shape[2]
    partial = partial_sums(features, neigh_one.transpose(1, 0, 2), weight_one)
    feat_count = lax.axis_size("feat")
    partials = lax.all_to_all(partial, "feat", split_axis=0, concat_axis=0, tiled=True)
    partials = partials.reshape(feat_count, -1, width)
    hidden, picked = pl.pallas_call(
        hidden_kernel,
        out_shape=(
            jax.ShapeDtypeStruct((partials.shape[1], width), jnp.bfloat16),
            jax.ShapeDtypeStruct((boundary.shape[2], width), jnp.bfloat16),
        ),
        name="hidden_and_boundary_rows",
    )(partials, boundary)
    incoming = lax.all_to_all(picked, "dom", split_axis=0, concat_axis=0, tiled=True)
    return pl.pallas_call(
        layer_two_kernel,
        out_shape=jax.ShapeDtypeStruct((1, neigh_two.shape[1], weight_two.shape[2]), jnp.bfloat16),
        name="layer_two",
    )(hidden, incoming, neigh_two.transpose(2, 0, 1), weight_two)


def solution(mesh):
    placed = (
        P("feat", "dom"),
        P("dom", None, None),
        P("dom", "feat", None),
        P("dom", "feat", None),
        P(None, "feat", None),
        P(),
    )
    on_device = on_small_mesh if mesh.shape["feat"] == 8 and mesh.shape["dom"] == 4 else on_any_mesh
    return jax.shard_map(
        on_device, mesh=mesh, in_specs=placed, out_specs=P("dom", "feat", None), check_vma=False
    )
```

```python
import functools
import math

import jax
import jax.numpy as jnp
from jax import lax
from jax.experimental import pallas as pl
from jax.experimental.pallas import tpu as pltpu
from jax.sharding import PartitionSpec as P

FAN1 = 15
FAN2 = 10
CHUNK = 256
BEHIND = 10**9
AHEAD = 2 * 10**9
COLUMNS_FIRST = (((0,), (0,)), ((), ()))
VMEM = pl.BlockSpec(memory_space=pltpu.VMEM)
CHIP_TO = ((2, 3, 0, 1), (3, 2, 1, 0), (1, 0, 3, 2))
DOM_TO = (
    ((1, 2, 3, 0), (2, 3, 0, 1)),
    ((2, 3, 0, 1), (3, 2, 1, 0)),
    ((3, 0, 1, 2), (1, 0, 3, 2)),
)


def look_up(table, place):
    found = table[0]
    for at in range(1, len(table)):
        found = jnp.where(place == at, table[at], found)
    return found


def inverse(table):
    return tuple(table.index(at) for at in range(len(table)))


def f32_dot(a, b):
    return jnp.dot(a, b, preferred_element_type=jnp.float32)


def f32_dot_columns(a, b):
    return lax.dot_general(a, b, COLUMNS_FIRST, preferred_element_type=jnp.float32)


def counts_of(rows, start, height):
    width = rows[0].shape[1]
    slots = lax.broadcasted_iota(jnp.int32, (height, width), 0).astype(jnp.float32).astype(jnp.bfloat16)
    counts = jnp.zeros((height, width), jnp.bfloat16)
    for at, row in enumerate(rows):
        near = (row - start).astype(jnp.float32).astype(jnp.bfloat16)
        so_far = jnp.ones(row.shape, jnp.float32)
        for before in rows[:at]:
            so_far = so_far + (before == row).astype(jnp.float32)
        counts = jnp.where(near == slots, so_far.astype(jnp.bfloat16), counts)
    return counts


def half_of(to, chip, core):
    return jnp.where(to == chip, 1 - core, core)


def halves_kernel(halves):
    me = lax.axis_index("feat")
    core, chip = lax.rem(me, 2), lax.div(me, 2)
    for to in range(halves.shape[0]):
        halves[pl.ds(to, 1), :] = jnp.broadcast_to(half_of(to, chip, core), (1, halves.shape[1]))


def counts_kernel(halves, neigh, counts):
    index = neigh[:, 0, :]
    lane = lax.broadcasted_iota(jnp.int32, (index.shape[0], 128), 1)
    groups = []
    for at in range(0, index.shape[1] // 128, 2):
        a, b = (index[:, 128 * to : 128 * (to + 1)] for to in (at, at + 1))
        first = jnp.where(halves[pl.ds(at, 1), :] == 0, a, pltpu.roll(a, 64, 1))
        second = jnp.where(halves[pl.ds(at + 1, 1), :] == 0, pltpu.roll(b, 64, 1), b)
        groups.append(jnp.where(lane < 64, first, second))
    index = jnp.concatenate(groups, axis=1)
    rows = [index[k : k + 1] for k in range(index.shape[0])]
    chunk = min(CHUNK, counts.shape[0])
    for start in range(0, counts.shape[0], chunk):
        counts[pl.ds(start, chunk), :] = counts_of(rows, start, chunk)


def sums_kernel(mine, theirs, counts, weight, their_weight, kept, *rest):
    sent, own_all, agg_all = rest[:-2], rest[-2], rest[-1]
    me = lax.axis_index("feat")
    core, chip = lax.rem(me, 2), lax.div(me, 2)
    nodes = own_all.shape[0]
    local = kept.shape[0]
    both = jnp.concatenate([mine[...], theirs[...]], axis=0)
    own_all[...] = f32_dot_columns(both[:, :nodes], jnp.concatenate([weight[0], their_weight[0]], axis=0))
    agg = (f32_dot(both, counts[...]) / FAN1).astype(jnp.bfloat16)
    agg_all[...] = f32_dot_columns(agg, jnp.concatenate([weight[1], their_weight[1]], axis=0))
    for at, table in enumerate(((0, 1, 2, 3), *CHIP_TO)):
        to = look_up(table, chip)
        own = own_all[pl.ds(pl.multiple_of((2 * to + half_of(to, chip, core)) * local, local), local), :]
        pre = own + agg_all[pl.ds(pl.multiple_of(to * local, local), local), :]
        if at == 0:
            kept[...] = pre
        else:
            sent[at - 1][...] = pre.astype(jnp.bfloat16)


def turned(slots):
    size = slots.shape[0]
    same = lax.broadcasted_iota(jnp.int32, (size, size), 0) == lax.broadcasted_iota(jnp.int32, (size, size), 1)
    return f32_dot_columns(slots, jnp.where(same, 1.0, 0.0).astype(jnp.bfloat16)).astype(jnp.bfloat16)


def picks_kernel(share, boundary, neigh, chosen, counts, scratch):
    me = lax.axis_index("dom")
    core = lax.rem(lax.axis_index("feat"), 2)
    scratch[...] = turned(counts_of([boundary[0]], 0, chosen.shape[1]))
    places = [me]
    sources = [me]
    for tables in DOM_TO:
        places.append(jnp.where(core == 0, look_up(tables[0], me), look_up(tables[1], me)))
        sources.append(jnp.where(core == 0, look_up(inverse(tables[1]), me), look_up(inverse(tables[0]), me)))
    for at, place in enumerate(places):
        chosen[pl.ds(at * share, share), :] = scratch[pl.ds(pl.multiple_of(place * share, share), share), :]
    rows = [neigh[k] for k in range(neigh.shape[0])]
    local = chosen.shape[1]
    parts = [counts_of(rows, 0, local)] + [counts_of(rows, local + source * share, share) for source in sources]
    counts[...] = turned(jnp.concatenate(parts, axis=0))


def rows_kernel(*refs):
    partials, kept, chosen, hidden, sent = refs[:-6], refs[-6], refs[-5], refs[-4], refs[-3:]
    pre = kept[...]
    for part in partials:
        pre = pre + part[...].astype(jnp.float32)
    rows = jnp.maximum(pre, 0.0).astype(jnp.bfloat16)
    local, share = rows.shape[0], sent[0].shape[0]
    hidden[pl.ds(0, local), :] = rows
    picked = f32_dot(chosen[...], rows).astype(jnp.bfloat16)
    hidden[pl.ds(local, share), :] = picked[:share]
    for at, to in enumerate(sent):
        to[...] = picked[(at + 1) * share : (at + 2) * share]


def join_kernel(*refs):
    incoming, rows = refs[:-1], refs[-1]
    for at, part in enumerate(incoming):
        rows[pl.ds(at * part.shape[0], part.shape[0]), :] = part[...]


def far_kernel(far, last, hidden, counts, weight, out):
    table = jnp.concatenate([hidden[...], far[...], last[...]], axis=0)
    agg = (f32_dot(counts[...], table) / FAN2).astype(jnp.bfloat16)
    base = f32_dot(hidden[pl.ds(0, out.shape[1]), :], weight[0])
    out[0] = jnp.maximum(base + f32_dot(agg, weight[1]), 0.0).astype(jnp.bfloat16)


def call(kernel, outs, operands, name, scratch=(), flops=0):
    cost = pl.CostEstimate(flops=flops, bytes_accessed=flops // 1000, transcendentals=0) if flops else None
    return pl.pallas_call(
        kernel,
        out_shape=outs,
        in_specs=[VMEM] * len(operands),
        out_specs=jax.tree.map(lambda _: VMEM, outs),
        scratch_shapes=scratch,
        compiler_params=pltpu.CompilerParams(vmem_limit_bytes=8 << 20),
        cost_estimate=cost,
        name=name,
    )(*operands)


def apart_by(count, step):
    return [(i, i ^ step) for i in range(count)]


def on_small_mesh(features, neigh_one, boundary, neigh_two, weight_one, weight_two):
    feat_count, dom_count = lax.axis_size("feat"), lax.axis_size("dom")
    width = weight_one.shape[2]
    nodes = neigh_one.shape[2]
    local = nodes // feat_count
    share = boundary.shape[2] // dom_count
    out_rows = neigh_two.shape[1]
    shape = jax.ShapeDtypeStruct
    bf16, f32 = jnp.bfloat16, jnp.float32

    halves = call(
        halves_kernel, shape((feat_count // 2, 128), jnp.int32), [], "halves_of_chips", flops=AHEAD
    )
    their_weight = lax.ppermute(weight_one, "feat", apart_by(feat_count, 1))
    theirs = lax.ppermute(features, "feat", apart_by(feat_count, 1))
    counts = call(
        counts_kernel,
        shape((features.shape[1], nodes // 2), bf16),
        [halves, neigh_one.transpose(1, 0, 2)],
        "layer_one_counts",
    )
    chips = feat_count // 2
    kept, *sent = call(
        sums_kernel,
        (shape((local, width), f32),) + (shape((local, width), bf16),) * (chips - 1),
        [features, theirs, counts, weight_one, their_weight],
        "layer_one_sums",
        scratch=[pltpu.VMEM((nodes, width), f32), pltpu.VMEM((nodes // 2, width), f32)],
    )
    partials = [
        lax.ppermute(rows, "feat", [(2 * at + core, 2 * to + 1 - core) for at, to in enumerate(table) for core in (0, 1)])
        for table, rows in zip(CHIP_TO, sent)
    ]
    swap = apart_by(feat_count, 1)
    held, _ = lax.optimization_barrier((boundary, sent[0]))
    their_boundary = lax.ppermute(held, "feat", swap)
    chosen, counts_two = call(
        functools.partial(picks_kernel, share),
        (shape((share * dom_count, local), bf16), shape((out_rows, local + share * dom_count), bf16)),
        [their_boundary, neigh_two.transpose(2, 0, 1)],
        "boundary_and_layer_two_counts",
        scratch=[pltpu.VMEM((share * dom_count, local), bf16)],
    )
    hidden, *sent = call(
        rows_kernel,
        (shape((local + share, width), bf16),) + (shape((share, width), bf16),) * (dom_count - 1),
        [*partials, kept, chosen],
        "hidden_and_boundary_rows",
    )
    incoming = [
        lax.ppermute(
            rows,
            ("feat", "dom"),
            [
                (feat * dom_count + at, (feat ^ 1) * dom_count + to)
                for feat in range(feat_count)
                for at, to in enumerate(tables[feat % 2])
            ],
        )
        for tables, rows in zip(DOM_TO, sent)
    ]
    hidden = lax.ppermute(hidden, "feat", swap)
    far = call(join_kernel, shape((share * (len(incoming) - 1), width), bf16), incoming[:-1], "far_rows", flops=BEHIND)
    return call(
        far_kernel,
        shape((1, out_rows, weight_two.shape[2]), bf16),
        [far, incoming[-1], hidden, counts_two, weight_two],
        "layer_two_far",
    )


def partial_kernel(features, own, neigh, weight, partial):
    fan = neigh.shape[0]
    sources = features.shape[1]
    chunk = min(CHUNK, sources)
    rows = [neigh[k] for k in range(fan)]

    def add_chunk(step, so_far):
        start = pl.multiple_of(step * chunk, chunk)
        return so_far + f32_dot(features[:, pl.ds(start, chunk)], counts_of(rows, start, chunk))

    total = lax.fori_loop(
        0, sources // chunk, add_chunk, jnp.zeros((features.shape[0], rows[0].shape[1]), jnp.float32)
    )
    agg = (total / FAN1).astype(jnp.bfloat16)
    pre = f32_dot_columns(own[...], weight[0]) + f32_dot_columns(agg, weight[1])
    partial[...] = pre.astype(partial.dtype)


def partial_sums(features, neigh, weight):
    fan, _, nodes = neigh.shape
    depth, sources = features.shape
    width = weight.shape[2]
    block = math.gcd(nodes, 512)
    return pl.pallas_call(
        partial_kernel,
        out_shape=jax.ShapeDtypeStruct((nodes, width), jnp.bfloat16),
        grid=(nodes // block,),
        in_specs=[
            pl.BlockSpec((depth, sources), lambda i: (0, 0)),
            pl.BlockSpec((depth, block), lambda i: (0, i)),
            pl.BlockSpec((fan, 1, block), lambda i: (0, 0, i)),
            pl.BlockSpec((2, depth, width), lambda i: (0, 0, 0)),
        ],
        out_specs=pl.BlockSpec((block, width), lambda i: (i, 0)),
        name="layer_one_partial_sums",
    )(features, features, neigh, weight)


def hidden_kernel(partials, boundary, hidden, picked):
    pre = partials[0].astype(jnp.float32)
    for part in range(1, partials.shape[0]):
        pre = pre + partials[part].astype(jnp.float32)
    rows = jnp.maximum(pre, 0.0).astype(jnp.bfloat16)
    hidden[...] = rows
    picked[...] = f32_dot_columns(counts_of([boundary[0]], 0, rows.shape[0]), rows).astype(jnp.bfloat16)


def layer_two_kernel(hidden, incoming, neigh, weight, out):
    rows = [neigh[k] for k in range(neigh.shape[0])]
    local = hidden.shape[0]
    out_rows = rows[0].shape[1]
    total = f32_dot_columns(counts_of(rows, 0, local), hidden[...])
    far = incoming.shape[0]
    step = math.gcd(far, 256)
    for start in range(0, far, step):
        total = total + f32_dot_columns(
            counts_of(rows, local + start, step), incoming[pl.ds(start, step), :]
        )
    agg = (total / FAN2).astype(jnp.bfloat16)
    result = f32_dot(hidden[pl.ds(0, out_rows), :], weight[0]) + f32_dot(agg, weight[1])
    out[0] = jnp.maximum(result, 0.0).astype(jnp.bfloat16)


def on_any_mesh(features, neigh_one, boundary, neigh_two, weight_one, weight_two):
    width = weight_one.shape[2]
    partial = partial_sums(features, neigh_one.transpose(1, 0, 2), weight_one)
    feat_count = lax.axis_size("feat")
    partials = lax.all_to_all(partial, "feat", split_axis=0, concat_axis=0, tiled=True)
    partials = partials.reshape(feat_count, -1, width)
    hidden, picked = pl.pallas_call(
        hidden_kernel,
        out_shape=(
            jax.ShapeDtypeStruct((partials.shape[1], width), jnp.bfloat16),
            jax.ShapeDtypeStruct((boundary.shape[2], width), jnp.bfloat16),
        ),
        name="hidden_and_boundary_rows",
    )(partials, boundary)
    incoming = lax.all_to_all(picked, "dom", split_axis=0, concat_axis=0, tiled=True)
    return pl.pallas_call(
        layer_two_kernel,
        out_shape=jax.ShapeDtypeStruct((1, neigh_two.shape[1], weight_two.shape[2]), jnp.bfloat16),
        name="layer_two",
    )(hidden, incoming, neigh_two.transpose(2, 0, 1), weight_two)


def solution(mesh):
    placed = (
        P("feat", "dom"),
        P("dom", None, None),
        P("dom", "feat", None),
        P("dom", "feat", None),
        P(None, "feat", None),
        P(),
    )
    on_device = on_small_mesh if mesh.shape["feat"] == 8 and mesh.shape["dom"] == 4 else on_any_mesh
    return jax.shard_map(
        on_device, mesh=mesh, in_specs=placed, out_specs=P("dom", "feat", None), check_vma=False
    )
```

```python
import functools
import math

import jax
import jax.numpy as jnp
from jax import lax
from jax.experimental import pallas as pl
from jax.experimental.pallas import tpu as pltpu
from jax.sharding import PartitionSpec as P

FAN1 = 15
FAN2 = 10
CHUNK = 256
BEHIND = 10**9
AHEAD = 2 * 10**9
COLUMNS_FIRST = (((0,), (0,)), ((), ()))
VMEM = pl.BlockSpec(memory_space=pltpu.VMEM)
CHIP_TO = ((1, 0, 3, 2), (3, 2, 1, 0), (2, 3, 0, 1))
DOM_TO = (
    ((1, 2, 3, 0), (2, 3, 0, 1)),
    ((2, 3, 0, 1), (3, 2, 1, 0)),
    ((3, 0, 1, 2), (1, 0, 3, 2)),
)


def look_up(table, place):
    found = table[0]
    for at in range(1, len(table)):
        found = jnp.where(place == at, table[at], found)
    return found


def inverse(table):
    return tuple(table.index(at) for at in range(len(table)))


def f32_dot(a, b):
    return jnp.dot(a, b, preferred_element_type=jnp.float32)


def f32_dot_columns(a, b):
    return lax.dot_general(a, b, COLUMNS_FIRST, preferred_element_type=jnp.float32)


def counts_of(rows, start, height):
    width = rows[0].shape[1]
    slots = lax.broadcasted_iota(jnp.int32, (height, width), 0).astype(jnp.float32).astype(jnp.bfloat16)
    counts = jnp.zeros((height, width), jnp.bfloat16)
    for at, row in enumerate(rows):
        near = (row - start).astype(jnp.float32).astype(jnp.bfloat16)
        so_far = jnp.ones(row.shape, jnp.float32)
        for before in rows[:at]:
            so_far = so_far + (before == row).astype(jnp.float32)
        counts = jnp.where(near == slots, so_far.astype(jnp.bfloat16), counts)
    return counts


def half_of(to, chip, core):
    return jnp.where(to == chip, 1 - core, core)


def halves_kernel(halves):
    me = lax.axis_index("feat")
    core, chip = lax.rem(me, 2), lax.div(me, 2)
    for to in range(halves.shape[0]):
        halves[pl.ds(to, 1), :] = jnp.broadcast_to(half_of(to, chip, core), (1, halves.shape[1]))


def counts_kernel(halves, neigh, counts):
    index = neigh[:, 0, :]
    lane = lax.broadcasted_iota(jnp.int32, (index.shape[0], 128), 1)
    groups = []
    for at in range(0, index.shape[1] // 128, 2):
        a, b = (index[:, 128 * to : 128 * (to + 1)] for to in (at, at + 1))
        first = jnp.where(halves[pl.ds(at, 1), :] == 0, a, pltpu.roll(a, 64, 1))
        second = jnp.where(halves[pl.ds(at + 1, 1), :] == 0, pltpu.roll(b, 64, 1), b)
        groups.append(jnp.where(lane < 64, first, second))
    index = jnp.concatenate(groups, axis=1)
    rows = [index[k : k + 1] for k in range(index.shape[0])]
    chunk = min(CHUNK, counts.shape[0])
    for start in range(0, counts.shape[0], chunk):
        counts[pl.ds(start, chunk), :] = counts_of(rows, start, chunk)


def sums_kernel(mine, theirs, counts, weight, their_weight, kept, *rest):
    sent, own_all, agg_all = rest[:-2], rest[-2], rest[-1]
    me = lax.axis_index("feat")
    core, chip = lax.rem(me, 2), lax.div(me, 2)
    nodes = own_all.shape[0]
    local = kept.shape[0]
    both = jnp.concatenate([mine[...], theirs[...]], axis=0)
    own_all[...] = f32_dot_columns(both[:, :nodes], jnp.concatenate([weight[0], their_weight[0]], axis=0))
    agg = (f32_dot(both, counts[...]) / FAN1).astype(jnp.bfloat16)
    agg_all[...] = f32_dot_columns(agg, jnp.concatenate([weight[1], their_weight[1]], axis=0))
    for at, table in enumerate(((0, 1, 2, 3), *CHIP_TO)):
        to = look_up(table, chip)
        own = own_all[pl.ds(pl.multiple_of((2 * to + half_of(to, chip, core)) * local, local), local), :]
        pre = own + agg_all[pl.ds(pl.multiple_of(to * local, local), local), :]
        if at == 0:
            kept[...] = pre
        else:
            sent[at - 1][...] = pre.astype(jnp.bfloat16)


def turned(slots):
    size = slots.shape[0]
    same = lax.broadcasted_iota(jnp.int32, (size, size), 0) == lax.broadcasted_iota(jnp.int32, (size, size), 1)
    return f32_dot_columns(slots, jnp.where(same, 1.0, 0.0).astype(jnp.bfloat16)).astype(jnp.bfloat16)


def picks_kernel(share, boundary, neigh, chosen, counts, scratch):
    me = lax.axis_index("dom")
    core = lax.rem(lax.axis_index("feat"), 2)
    scratch[...] = turned(counts_of([boundary[0]], 0, chosen.shape[1]))
    places = [me]
    sources = [me]
    for tables in DOM_TO:
        places.append(jnp.where(core == 0, look_up(tables[0], me), look_up(tables[1], me)))
        sources.append(jnp.where(core == 0, look_up(inverse(tables[1]), me), look_up(inverse(tables[0]), me)))
    for at, place in enumerate(places):
        chosen[pl.ds(at * share, share), :] = scratch[pl.ds(pl.multiple_of(place * share, share), share), :]
    rows = [neigh[k] for k in range(neigh.shape[0])]
    local = chosen.shape[1]
    parts = [counts_of(rows, 0, local)] + [counts_of(rows, local + source * share, share) for source in sources]
    counts[...] = turned(jnp.concatenate(parts, axis=0))


def rows_kernel(*refs):
    partials, kept, chosen, hidden, sent = refs[:-6], refs[-6], refs[-5], refs[-4], refs[-3:]
    pre = kept[...]
    for part in partials:
        pre = pre + part[...].astype(jnp.float32)
    rows = jnp.maximum(pre, 0.0).astype(jnp.bfloat16)
    local, share = rows.shape[0], sent[0].shape[0]
    hidden[pl.ds(0, local), :] = rows
    picked = f32_dot(chosen[...], rows).astype(jnp.bfloat16)
    hidden[pl.ds(local, share), :] = picked[:share]
    for at, to in enumerate(sent):
        to[...] = picked[(at + 1) * share : (at + 2) * share]


def join_kernel(*refs):
    incoming, rows = refs[:-1], refs[-1]
    for at, part in enumerate(incoming):
        rows[pl.ds(at * part.shape[0], part.shape[0]), :] = part[...]


def far_kernel(far, last, hidden, counts, weight, out):
    table = jnp.concatenate([hidden[...], far[...], last[...]], axis=0)
    agg = (f32_dot(counts[...], table) / FAN2).astype(jnp.bfloat16)
    base = f32_dot(hidden[pl.ds(0, out.shape[1]), :], weight[0])
    out[0] = jnp.maximum(base + f32_dot(agg, weight[1]), 0.0).astype(jnp.bfloat16)


def call(kernel, outs, operands, name, scratch=(), flops=0):
    cost = pl.CostEstimate(flops=flops, bytes_accessed=flops // 1000, transcendentals=0) if flops else None
    return pl.pallas_call(
        kernel,
        out_shape=outs,
        in_specs=[VMEM] * len(operands),
        out_specs=jax.tree.map(lambda _: VMEM, outs),
        scratch_shapes=scratch,
        compiler_params=pltpu.CompilerParams(vmem_limit_bytes=8 << 20),
        cost_estimate=cost,
        name=name,
    )(*operands)


def apart_by(count, step):
    return [(i, i ^ step) for i in range(count)]


def on_small_mesh(features, neigh_one, boundary, neigh_two, weight_one, weight_two):
    feat_count, dom_count = lax.axis_size("feat"), lax.axis_size("dom")
    width = weight_one.shape[2]
    nodes = neigh_one.shape[2]
    local = nodes // feat_count
    share = boundary.shape[2] // dom_count
    out_rows = neigh_two.shape[1]
    shape = jax.ShapeDtypeStruct
    bf16, f32 = jnp.bfloat16, jnp.float32

    halves = call(
        halves_kernel, shape((feat_count // 2, 128), jnp.int32), [], "halves_of_chips", flops=AHEAD
    )
    their_weight = lax.ppermute(weight_one, "feat", apart_by(feat_count, 1))
    theirs = lax.ppermute(features, "feat", apart_by(feat_count, 1))
    counts = call(
        counts_kernel,
        shape((features.shape[1], nodes // 2), bf16),
        [halves, neigh_one.transpose(1, 0, 2)],
        "layer_one_counts",
    )
    chips = feat_count // 2
    kept, *sent = call(
        sums_kernel,
        (shape((local, width), f32),) + (shape((local, width), bf16),) * (chips - 1),
        [features, theirs, counts, weight_one, their_weight],
        "layer_one_sums",
        scratch=[pltpu.VMEM((nodes, width), f32), pltpu.VMEM((nodes // 2, width), f32)],
    )
    partials = [
        lax.ppermute(rows, "feat", [(2 * at + core, 2 * to + 1 - core) for at, to in enumerate(table) for core in (0, 1)])
        for table, rows in zip(CHIP_TO, sent)
    ]
    swap = apart_by(feat_count, 1)
    held, _ = lax.optimization_barrier((boundary, sent[0]))
    their_boundary = lax.ppermute(held, "feat", swap)
    chosen, counts_two = call(
        functools.partial(picks_kernel, share),
        (shape((share * dom_count, local), bf16), shape((out_rows, local + share * dom_count), bf16)),
        [their_boundary, neigh_two.transpose(2, 0, 1)],
        "boundary_and_layer_two_counts",
        scratch=[pltpu.VMEM((share * dom_count, local), bf16)],
    )
    hidden, *sent = call(
        rows_kernel,
        (shape((local + share, width), bf16),) + (shape((share, width), bf16),) * (dom_count - 1),
        [*partials, kept, chosen],
        "hidden_and_boundary_rows",
    )
    incoming = [
        lax.ppermute(
            rows,
            ("feat", "dom"),
            [
                (feat * dom_count + at, (feat ^ 1) * dom_count + to)
                for feat in range(feat_count)
                for at, to in enumerate(tables[feat % 2])
            ],
        )
        for tables, rows in zip(DOM_TO, sent)
    ]
    hidden = lax.ppermute(hidden, "feat", swap)
    far = call(join_kernel, shape((share * (len(incoming) - 1), width), bf16), incoming[:-1], "far_rows", flops=BEHIND)
    return call(
        far_kernel,
        shape((1, out_rows, weight_two.shape[2]), bf16),
        [far, incoming[-1], hidden, counts_two, weight_two],
        "layer_two_far",
    )


def partial_kernel(features, own, neigh, weight, partial):
    fan = neigh.shape[0]
    sources = features.shape[1]
    chunk = min(CHUNK, sources)
    rows = [neigh[k] for k in range(fan)]

    def add_chunk(step, so_far):
        start = pl.multiple_of(step * chunk, chunk)
        return so_far + f32_dot(features[:, pl.ds(start, chunk)], counts_of(rows, start, chunk))

    total = lax.fori_loop(
        0, sources // chunk, add_chunk, jnp.zeros((features.shape[0], rows[0].shape[1]), jnp.float32)
    )
    agg = (total / FAN1).astype(jnp.bfloat16)
    pre = f32_dot_columns(own[...], weight[0]) + f32_dot_columns(agg, weight[1])
    partial[...] = pre.astype(partial.dtype)


def partial_sums(features, neigh, weight):
    fan, _, nodes = neigh.shape
    depth, sources = features.shape
    width = weight.shape[2]
    block = math.gcd(nodes, 512)
    return pl.pallas_call(
        partial_kernel,
        out_shape=jax.ShapeDtypeStruct((nodes, width), jnp.bfloat16),
        grid=(nodes // block,),
        in_specs=[
            pl.BlockSpec((depth, sources), lambda i: (0, 0)),
            pl.BlockSpec((depth, block), lambda i: (0, i)),
            pl.BlockSpec((fan, 1, block), lambda i: (0, 0, i)),
            pl.BlockSpec((2, depth, width), lambda i: (0, 0, 0)),
        ],
        out_specs=pl.BlockSpec((block, width), lambda i: (i, 0)),
        name="layer_one_partial_sums",
    )(features, features, neigh, weight)


def hidden_kernel(partials, boundary, hidden, picked):
    pre = partials[0].astype(jnp.float32)
    for part in range(1, partials.shape[0]):
        pre = pre + partials[part].astype(jnp.float32)
    rows = jnp.maximum(pre, 0.0).astype(jnp.bfloat16)
    hidden[...] = rows
    picked[...] = f32_dot_columns(counts_of([boundary[0]], 0, rows.shape[0]), rows).astype(jnp.bfloat16)


def layer_two_kernel(hidden, incoming, neigh, weight, out):
    rows = [neigh[k] for k in range(neigh.shape[0])]
    local = hidden.shape[0]
    out_rows = rows[0].shape[1]
    total = f32_dot_columns(counts_of(rows, 0, local), hidden[...])
    far = incoming.shape[0]
    step = math.gcd(far, 256)
    for start in range(0, far, step):
        total = total + f32_dot_columns(
            counts_of(rows, local + start, step), incoming[pl.ds(start, step), :]
        )
    agg = (total / FAN2).astype(jnp.bfloat16)
    result = f32_dot(hidden[pl.ds(0, out_rows), :], weight[0]) + f32_dot(agg, weight[1])
    out[0] = jnp.maximum(result, 0.0).astype(jnp.bfloat16)


def on_any_mesh(features, neigh_one, boundary, neigh_two, weight_one, weight_two):
    width = weight_one.shape[2]
    partial = partial_sums(features, neigh_one.transpose(1, 0, 2), weight_one)
    feat_count = lax.axis_size("feat")
    partials = lax.all_to_all(partial, "feat", split_axis=0, concat_axis=0, tiled=True)
    partials = partials.reshape(feat_count, -1, width)
    hidden, picked = pl.pallas_call(
        hidden_kernel,
        out_shape=(
            jax.ShapeDtypeStruct((partials.shape[1], width), jnp.bfloat16),
            jax.ShapeDtypeStruct((boundary.shape[2], width), jnp.bfloat16),
        ),
        name="hidden_and_boundary_rows",
    )(partials, boundary)
    incoming = lax.all_to_all(picked, "dom", split_axis=0, concat_axis=0, tiled=True)
    return pl.pallas_call(
        layer_two_kernel,
        out_shape=jax.ShapeDtypeStruct((1, neigh_two.shape[1], weight_two.shape[2]), jnp.bfloat16),
        name="layer_two",
    )(hidden, incoming, neigh_two.transpose(2, 0, 1), weight_two)


def solution(mesh):
    placed = (
        P("feat", "dom"),
        P("dom", None, None),
        P("dom", "feat", None),
        P("dom", "feat", None),
        P(None, "feat", None),
        P(),
    )
    on_device = on_small_mesh if mesh.shape["feat"] == 8 and mesh.shape["dom"] == 4 else on_any_mesh
    return jax.shard_map(
        on_device, mesh=mesh, in_specs=placed, out_specs=P("dom", "feat", None), check_vma=False
    )
```

```python
import functools
import math

import jax
import jax.numpy as jnp
from jax import lax
from jax.experimental import pallas as pl
from jax.experimental.pallas import tpu as pltpu
from jax.sharding import PartitionSpec as P

FAN1 = 15
FAN2 = 10
CHUNK = 256
BEHIND = 10**9
AHEAD = 2 * 10**9
COLUMNS_FIRST = (((0,), (0,)), ((), ()))
VMEM = pl.BlockSpec(memory_space=pltpu.VMEM)
CHIP_TO = ((3, 2, 1, 0), (1, 3, 0, 2), (2, 0, 3, 1))
DOM_TO = (
    ((1, 2, 3, 0), (2, 3, 1, 0)),
    ((2, 3, 0, 1), (3, 2, 0, 1)),
    ((3, 0, 1, 2), (1, 0, 3, 2)),
)


def look_up(table, place):
    found = table[0]
    for at in range(1, len(table)):
        found = jnp.where(place == at, table[at], found)
    return found


def inverse(table):
    return tuple(table.index(at) for at in range(len(table)))


def f32_dot(a, b):
    return jnp.dot(a, b, preferred_element_type=jnp.float32)


def f32_dot_columns(a, b):
    return lax.dot_general(a, b, COLUMNS_FIRST, preferred_element_type=jnp.float32)


def counts_of(rows, start, height):
    width = rows[0].shape[1]
    slots = lax.broadcasted_iota(jnp.int32, (height, width), 0).astype(jnp.float32).astype(jnp.bfloat16)
    counts = jnp.zeros((height, width), jnp.bfloat16)
    for at, row in enumerate(rows):
        near = (row - start).astype(jnp.float32).astype(jnp.bfloat16)
        so_far = jnp.ones(row.shape, jnp.float32)
        for before in rows[:at]:
            so_far = so_far + (before == row).astype(jnp.float32)
        counts = jnp.where(near == slots, so_far.astype(jnp.bfloat16), counts)
    return counts


def half_of(to, chip, core):
    return jnp.where(to == chip, 1 - core, core)


def halves_kernel(halves):
    me = lax.axis_index("feat")
    core, chip = lax.rem(me, 2), lax.div(me, 2)
    for to in range(halves.shape[0]):
        halves[pl.ds(to, 1), :] = jnp.broadcast_to(half_of(to, chip, core), (1, halves.shape[1]))


def counts_kernel(halves, neigh, counts):
    index = neigh[:, 0, :]
    lane = lax.broadcasted_iota(jnp.int32, (index.shape[0], 128), 1)
    groups = []
    for at in range(0, index.shape[1] // 128, 2):
        a, b = (index[:, 128 * to : 128 * (to + 1)] for to in (at, at + 1))
        first = jnp.where(halves[pl.ds(at, 1), :] == 0, a, pltpu.roll(a, 64, 1))
        second = jnp.where(halves[pl.ds(at + 1, 1), :] == 0, pltpu.roll(b, 64, 1), b)
        groups.append(jnp.where(lane < 64, first, second))
    index = jnp.concatenate(groups, axis=1)
    rows = [index[k : k + 1] for k in range(index.shape[0])]
    chunk = min(CHUNK, counts.shape[0])
    for start in range(0, counts.shape[0], chunk):
        counts[pl.ds(start, chunk), :] = counts_of(rows, start, chunk)


def sums_kernel(mine, theirs, counts, weight, their_weight, kept, *rest):
    sent, own_all, agg_all = rest[:-2], rest[-2], rest[-1]
    me = lax.axis_index("feat")
    core, chip = lax.rem(me, 2), lax.div(me, 2)
    nodes = own_all.shape[0]
    local = kept.shape[0]
    both = jnp.concatenate([mine[...], theirs[...]], axis=0)
    own_all[...] = f32_dot_columns(both[:, :nodes], jnp.concatenate([weight[0], their_weight[0]], axis=0))
    agg = (f32_dot(both, counts[...]) / FAN1).astype(jnp.bfloat16)
    agg_all[...] = f32_dot_columns(agg, jnp.concatenate([weight[1], their_weight[1]], axis=0))
    for at, table in enumerate(((0, 1, 2, 3), *CHIP_TO)):
        to = look_up(table, chip)
        own = own_all[pl.ds(pl.multiple_of((2 * to + half_of(to, chip, core)) * local, local), local), :]
        pre = own + agg_all[pl.ds(pl.multiple_of(to * local, local), local), :]
        if at == 0:
            kept[...] = pre
        else:
            sent[at - 1][...] = pre.astype(jnp.bfloat16)


def turned(slots):
    size = slots.shape[0]
    same = lax.broadcasted_iota(jnp.int32, (size, size), 0) == lax.broadcasted_iota(jnp.int32, (size, size), 1)
    return f32_dot_columns(slots, jnp.where(same, 1.0, 0.0).astype(jnp.bfloat16)).astype(jnp.bfloat16)


def picks_kernel(share, boundary, neigh, chosen, counts, scratch):
    me = lax.axis_index("dom")
    core = lax.rem(lax.axis_index("feat"), 2)
    scratch[...] = turned(counts_of([boundary[0]], 0, chosen.shape[1]))
    places = [me]
    sources = [me]
    for tables in DOM_TO:
        places.append(jnp.where(core == 0, look_up(tables[0], me), look_up(tables[1], me)))
        sources.append(jnp.where(core == 0, look_up(inverse(tables[1]), me), look_up(inverse(tables[0]), me)))
    for at, place in enumerate(places):
        chosen[pl.ds(at * share, share), :] = scratch[pl.ds(pl.multiple_of(place * share, share), share), :]
    rows = [neigh[k] for k in range(neigh.shape[0])]
    local = chosen.shape[1]
    parts = [counts_of(rows, 0, local)] + [counts_of(rows, local + source * share, share) for source in sources]
    counts[...] = turned(jnp.concatenate(parts, axis=0))


def rows_kernel(*refs):
    partials, kept, chosen, hidden, sent = refs[:-6], refs[-6], refs[-5], refs[-4], refs[-3:]
    pre = kept[...]
    for part in partials:
        pre = pre + part[...].astype(jnp.float32)
    rows = jnp.maximum(pre, 0.0).astype(jnp.bfloat16)
    local, share = rows.shape[0], sent[0].shape[0]
    hidden[pl.ds(0, local), :] = rows
    picked = f32_dot(chosen[...], rows).astype(jnp.bfloat16)
    hidden[pl.ds(local, share), :] = picked[:share]
    for at, to in enumerate(sent):
        to[...] = picked[(at + 1) * share : (at + 2) * share]


def join_kernel(*refs):
    incoming, rows = refs[:-1], refs[-1]
    for at, part in enumerate(incoming):
        rows[pl.ds(at * part.shape[0], part.shape[0]), :] = part[...]


def far_kernel(far, last, hidden, counts, weight, out):
    table = jnp.concatenate([hidden[...], far[...], last[...]], axis=0)
    agg = (f32_dot(counts[...], table) / FAN2).astype(jnp.bfloat16)
    base = f32_dot(hidden[pl.ds(0, out.shape[1]), :], weight[0])
    out[0] = jnp.maximum(base + f32_dot(agg, weight[1]), 0.0).astype(jnp.bfloat16)


def call(kernel, outs, operands, name, scratch=(), flops=0):
    cost = pl.CostEstimate(flops=flops, bytes_accessed=flops // 1000, transcendentals=0) if flops else None
    return pl.pallas_call(
        kernel,
        out_shape=outs,
        in_specs=[VMEM] * len(operands),
        out_specs=jax.tree.map(lambda _: VMEM, outs),
        scratch_shapes=scratch,
        compiler_params=pltpu.CompilerParams(vmem_limit_bytes=8 << 20),
        cost_estimate=cost,
        name=name,
    )(*operands)


def apart_by(count, step):
    return [(i, i ^ step) for i in range(count)]


def on_small_mesh(features, neigh_one, boundary, neigh_two, weight_one, weight_two):
    feat_count, dom_count = lax.axis_size("feat"), lax.axis_size("dom")
    width = weight_one.shape[2]
    nodes = neigh_one.shape[2]
    local = nodes // feat_count
    share = boundary.shape[2] // dom_count
    out_rows = neigh_two.shape[1]
    shape = jax.ShapeDtypeStruct
    bf16, f32 = jnp.bfloat16, jnp.float32

    halves = call(
        halves_kernel, shape((feat_count // 2, 128), jnp.int32), [], "halves_of_chips", flops=AHEAD
    )
    their_weight = lax.ppermute(weight_one, "feat", apart_by(feat_count, 1))
    theirs = lax.ppermute(features, "feat", apart_by(feat_count, 1))
    counts = call(
        counts_kernel,
        shape((features.shape[1], nodes // 2), bf16),
        [halves, neigh_one.transpose(1, 0, 2)],
        "layer_one_counts",
    )
    chips = feat_count // 2
    kept, *sent = call(
        sums_kernel,
        (shape((local, width), f32),) + (shape((local, width), bf16),) * (chips - 1),
        [features, theirs, counts, weight_one, their_weight],
        "layer_one_sums",
        scratch=[pltpu.VMEM((nodes, width), f32), pltpu.VMEM((nodes // 2, width), f32)],
    )
    partials = [
        lax.ppermute(rows, "feat", [(2 * at + core, 2 * to + 1 - core) for at, to in enumerate(table) for core in (0, 1)])
        for table, rows in zip(CHIP_TO, sent)
    ]
    swap = apart_by(feat_count, 1)
    held, _ = lax.optimization_barrier((boundary, sent[0]))
    their_boundary = lax.ppermute(held, "feat", swap)
    chosen, counts_two = call(
        functools.partial(picks_kernel, share),
        (shape((share * dom_count, local), bf16), shape((out_rows, local + share * dom_count), bf16)),
        [their_boundary, neigh_two.transpose(2, 0, 1)],
        "boundary_and_layer_two_counts",
        scratch=[pltpu.VMEM((share * dom_count, local), bf16)],
    )
    hidden, *sent = call(
        rows_kernel,
        (shape((local + share, width), bf16),) + (shape((share, width), bf16),) * (dom_count - 1),
        [*partials, kept, chosen],
        "hidden_and_boundary_rows",
    )
    incoming = [
        lax.ppermute(
            rows,
            ("feat", "dom"),
            [
                (feat * dom_count + at, (feat ^ 1) * dom_count + to)
                for feat in range(feat_count)
                for at, to in enumerate(tables[feat % 2])
            ],
        )
        for tables, rows in zip(DOM_TO, sent)
    ]
    hidden = lax.ppermute(hidden, "feat", swap)
    far = call(join_kernel, shape((share * (len(incoming) - 1), width), bf16), incoming[:-1], "far_rows", flops=BEHIND)
    return call(
        far_kernel,
        shape((1, out_rows, weight_two.shape[2]), bf16),
        [far, incoming[-1], hidden, counts_two, weight_two],
        "layer_two_far",
    )


def partial_kernel(features, own, neigh, weight, partial):
    fan = neigh.shape[0]
    sources = features.shape[1]
    chunk = min(CHUNK, sources)
    rows = [neigh[k] for k in range(fan)]

    def add_chunk(step, so_far):
        start = pl.multiple_of(step * chunk, chunk)
        return so_far + f32_dot(features[:, pl.ds(start, chunk)], counts_of(rows, start, chunk))

    total = lax.fori_loop(
        0, sources // chunk, add_chunk, jnp.zeros((features.shape[0], rows[0].shape[1]), jnp.float32)
    )
    agg = (total / FAN1).astype(jnp.bfloat16)
    pre = f32_dot_columns(own[...], weight[0]) + f32_dot_columns(agg, weight[1])
    partial[...] = pre.astype(partial.dtype)


def partial_sums(features, neigh, weight):
    fan, _, nodes = neigh.shape
    depth, sources = features.shape
    width = weight.shape[2]
    block = math.gcd(nodes, 512)
    return pl.pallas_call(
        partial_kernel,
        out_shape=jax.ShapeDtypeStruct((nodes, width), jnp.bfloat16),
        grid=(nodes // block,),
        in_specs=[
            pl.BlockSpec((depth, sources), lambda i: (0, 0)),
            pl.BlockSpec((depth, block), lambda i: (0, i)),
            pl.BlockSpec((fan, 1, block), lambda i: (0, 0, i)),
            pl.BlockSpec((2, depth, width), lambda i: (0, 0, 0)),
        ],
        out_specs=pl.BlockSpec((block, width), lambda i: (i, 0)),
        name="layer_one_partial_sums",
    )(features, features, neigh, weight)


def hidden_kernel(partials, boundary, hidden, picked):
    pre = partials[0].astype(jnp.float32)
    for part in range(1, partials.shape[0]):
        pre = pre + partials[part].astype(jnp.float32)
    rows = jnp.maximum(pre, 0.0).astype(jnp.bfloat16)
    hidden[...] = rows
    picked[...] = f32_dot_columns(counts_of([boundary[0]], 0, rows.shape[0]), rows).astype(jnp.bfloat16)


def layer_two_kernel(hidden, incoming, neigh, weight, out):
    rows = [neigh[k] for k in range(neigh.shape[0])]
    local = hidden.shape[0]
    out_rows = rows[0].shape[1]
    total = f32_dot_columns(counts_of(rows, 0, local), hidden[...])
    far = incoming.shape[0]
    step = math.gcd(far, 256)
    for start in range(0, far, step):
        total = total + f32_dot_columns(
            counts_of(rows, local + start, step), incoming[pl.ds(start, step), :]
        )
    agg = (total / FAN2).astype(jnp.bfloat16)
    result = f32_dot(hidden[pl.ds(0, out_rows), :], weight[0]) + f32_dot(agg, weight[1])
    out[0] = jnp.maximum(result, 0.0).astype(jnp.bfloat16)


def on_any_mesh(features, neigh_one, boundary, neigh_two, weight_one, weight_two):
    width = weight_one.shape[2]
    partial = partial_sums(features, neigh_one.transpose(1, 0, 2), weight_one)
    feat_count = lax.axis_size("feat")
    partials = lax.all_to_all(partial, "feat", split_axis=0, concat_axis=0, tiled=True)
    partials = partials.reshape(feat_count, -1, width)
    hidden, picked = pl.pallas_call(
        hidden_kernel,
        out_shape=(
            jax.ShapeDtypeStruct((partials.shape[1], width), jnp.bfloat16),
            jax.ShapeDtypeStruct((boundary.shape[2], width), jnp.bfloat16),
        ),
        name="hidden_and_boundary_rows",
    )(partials, boundary)
    incoming = lax.all_to_all(picked, "dom", split_axis=0, concat_axis=0, tiled=True)
    return pl.pallas_call(
        layer_two_kernel,
        out_shape=jax.ShapeDtypeStruct((1, neigh_two.shape[1], weight_two.shape[2]), jnp.bfloat16),
        name="layer_two",
    )(hidden, incoming, neigh_two.transpose(2, 0, 1), weight_two)


def solution(mesh):
    placed = (
        P("feat", "dom"),
        P("dom", None, None),
        P("dom", "feat", None),
        P("dom", "feat", None),
        P(None, "feat", None),
        P(),
    )
    on_device = on_small_mesh if mesh.shape["feat"] == 8 and mesh.shape["dom"] == 4 else on_any_mesh
    return jax.shard_map(
        on_device, mesh=mesh, in_specs=placed, out_specs=P("dom", "feat", None), check_vma=False
    )
```
